32 devices in a mesh: aux: 4 (over z), occ: 8 (over y, x, core).
Axes of the slice: x: 2, y: 2, z: 4, core: 2. Of those that a mesh axis runs over, the one named last changes fastest.
Arguments:
- half_ints: bfloat16 [1024, 128, 1024], P('aux', 'occ'), may hold values from -1 to 1
- block_mask: int32 [16, 128], P('aux', 'occ'), may hold values 0 or 1
- vir_coef: bfloat16 [1024, 2048], replicated, may hold values from -0.1875 to 0.1875
- domains: int32 [128, 512], replicated, may hold values from 0 to 2047, as said below
- vir_energy: float32 [2048], replicated, may hold values from 0.5 to 3
- occ_energy: float32 [128], replicated, may hold values from -3 to -0.5
- pair_count: int32 [8, 4], P('occ', 'aux'), may hold values from 2 to 16, as said below
- pair_code: int32 [8, 4, 16], P('occ', 'aux'), may hold values from 0 to 63, as said below
Outputs:
- density: bfloat16 [1024, 128, 512], P('aux', 'occ')
The draws below stay inside these ranges and needn't reach their ends.
Inputs may be any that keep to these rules, and one draw needn't show every extreme that they name: `domains`: each row names 512 distinct virtual orbitals. `pair_count`: some block holds exactly 16 live pairs. `pair_code`: the entries of one block's list are distinct.
All inputs are finite; a program needn't handle non-finite values. No bound on the sum of `block_mask` on one device may be relied on, other than what follows from the above.
Results may differ from the reference program's by a relative error of at most 0.0075.
Values may be sent and summed in bfloat16 or wider, within the bound.
No kernel may reach another device: no remote copies, remote signals or barrier semaphores. Data moves between devices by JAX's collectives and lax.ppermute only.
A program may use at most 128 MiB of HBM per device.

```python
import jax
import jax.numpy as jnp
from jax import lax

AUX = 1024
NVIR = 512
NBAS = 1024
NVALL = 2048
BLK = 64
OCC_DEV = 4
PARTNERS = 4
PAIR_CAP = 16
NOCC = 128
NBLK = 16
OCC_GROUPS = 8
AUX_GROUPS = 4
N_AUX = 4
N_OCC = 8


def draw_domains(key, part):
    keys = jax.random.split(jax.random.fold_in(key, 31), NOCC)

    def one_row(row_key):
        return jax.random.permutation(row_key, NVALL)[:NVIR]
    return jax.vmap(one_row)(keys).astype(jnp.int32)


def draw_pair_count(key, part):
    first = jax.random.fold_in(key, 11)
    second = jax.random.fold_in(key, 12)
    draws = jax.random.randint(first, (OCC_GROUPS * AUX_GROUPS,), 0, PAIR_CAP)
    counts = jnp.minimum(2 + draws * draws // PAIR_CAP, PAIR_CAP)
    chosen = jax.random.randint(second, (), 0, OCC_GROUPS * AUX_GROUPS)
    counts = counts.at[chosen].set(PAIR_CAP)
    return counts.reshape(OCC_GROUPS, AUX_GROUPS).astype(jnp.int32)


def draw_pair_code(key, part):
    keys = jax.random.split(jax.random.fold_in(key, 21), OCC_GROUPS * AUX_GROUPS)

    def one_list(list_key):
        return jax.random.permutation(list_key, PARTNERS * OCC_DEV * OCC_DEV)[:PAIR_CAP]
    codes = jax.vmap(one_list)(keys)
    return codes.reshape(OCC_GROUPS, AUX_GROUPS, PAIR_CAP).astype(jnp.int32)


def touch_ends(drawn, stream_key, least, high):
    dims = drawn.shape
    spot = [jax.random.randint(jax.random.fold_in(stream_key, axis), (), 0, dims[axis]) for axis in range(len(dims))]
    drawn = drawn.at[tuple(spot)].set(least)
    longest = dims.index(max(dims))
    spot[longest] = (spot[longest] + 1) % dims[longest]
    return drawn.at[tuple(spot)].set(high)


def block_scale(own_key, dims, pieces, least, largest):
    loudness, own = 1.0, jax.random.fold_in(own_key, 6)
    for position, shards_of in pieces:
        steps = jnp.exp(jax.random.uniform(jax.random.fold_in(own, position), (shards_of,), jnp.float32, least / len(pieces), largest / len(pieces)))
        loudness = loudness * jnp.repeat(steps, dims[position] // shards_of).reshape([-1 if axis == position else 1 for axis in range(len(dims))])
    return loudness


def bell_draw(own_key, extent, scale, reach, shards=(), kind=jnp.bfloat16):
    drawn = jax.random.normal(own_key, extent, jnp.float32) * scale
    if len(shards) > 0:
        drawn = block_scale(own_key, extent, shards, -0.22, 0.18) * drawn
    return jnp.clip(drawn, min=-reach, max=reach).astype(kind)


def setup_inputs(seed: int = 0) -> dict:
    seeds = jax.random.split(jax.random.key(seed), 9)
    return {
        "half_ints": bell_draw(seeds[0], (AUX, NOCC, NBAS), 0.16, 1.0, ((0, 4), (1, 8))),
        "block_mask": touch_ends((jax.random.randint(seeds[1], (NBLK, NOCC), 0, 4) < 3).astype(jnp.int32), jax.random.fold_in(seeds[1], 1), 0, 1),
        "vir_coef": bell_draw(seeds[2], (NBAS, NVALL), NBAS ** -0.5, 0.1875),
        "domains": draw_domains(jax.random.fold_in(seeds[8], 71), 0),
        "vir_energy": jnp.clip(jax.random.uniform(seeds[4], (NVALL,), jnp.float32, 0.5, 3.0), 0.5, 3.0),
        "occ_energy": jnp.clip(jax.random.uniform(seeds[5], (NOCC,), jnp.float32, -3.0, -0.5), -3.0, -0.5),
        "pair_count": draw_pair_count(jax.random.fold_in(seeds[8], 71), 0),
        "pair_code": draw_pair_code(jax.random.fold_in(seeds[8], 71), 0),
    }


def reference(half_ints, block_mask, vir_coef, domains, vir_energy, occ_energy, pair_count, pair_code):
    row_mask = jnp.repeat(block_mask, BLK, axis=0).astype(jnp.bfloat16)

    def transform(orbital):
        columns = jnp.take(vir_coef, domains[orbital], axis=1)
        masked = half_ints[:, orbital, :] * row_mask[:, orbital][:, None]
        return jnp.dot(masked, columns, preferred_element_type=jnp.float32).astype(jnp.bfloat16)

    coupled = lax.map(transform, jnp.arange(NOCC, dtype=jnp.int32))
    span = PARTNERS * OCC_DEV

    def device_block(device):
        occ_pos = device // N_AUX
        aux_pos = device % N_AUX
        blocks = []
        dom_rows = []
        occ_rows = []
        for offset in range(PARTNERS):
            start = ((((occ_pos + offset) % N_OCC) * N_AUX + aux_pos) * OCC_DEV).astype(jnp.int32)
            blocks.append(lax.dynamic_slice_in_dim(coupled, start, OCC_DEV, 0))
            dom_rows.append(lax.dynamic_slice_in_dim(domains, start, OCC_DEV, 0))
            occ_rows.append(lax.dynamic_slice_in_dim(occ_energy, start, OCC_DEV, 0))
        partners = jnp.concatenate(blocks, axis=0)
        partner_vir = jnp.take(vir_energy, jnp.concatenate(dom_rows, axis=0))
        partner_occ = jnp.concatenate(occ_rows, axis=0)
        codes = pair_code[occ_pos, aux_pos]

        def pair_step(slot, gamma):
            code = codes[slot]
            own_slot = code // span
            partner_slot = code % span
            own_rows = partners[own_slot]
            partner_rows = partners[partner_slot]
            exchange = lax.dot_general(own_rows, partner_rows, (((0,), (0,)), ((), ())), preferred_element_type=jnp.float32)
            denom = partner_vir[own_slot][:, None] + partner_vir[partner_slot][None, :] - partner_occ[own_slot] - partner_occ[partner_slot]
            amplitude = (exchange / denom).astype(jnp.bfloat16)
            contrib = lax.dot_general(partner_rows, amplitude, (((1,), (1,)), ((), ())), preferred_element_type=jnp.float32)
            current = lax.dynamic_index_in_dim(gamma, own_slot, 0, keepdims=True)
            return lax.dynamic_update_index_in_dim(gamma, current + contrib[None], own_slot, 0)

        gamma = jnp.zeros((OCC_DEV, AUX, NVIR), jnp.float32)
        gamma = lax.fori_loop(0, pair_count[occ_pos, aux_pos], pair_step, gamma)
        return gamma.astype(jnp.bfloat16)

    result = lax.map(device_block, jnp.arange(N_OCC * N_AUX, dtype=jnp.int32))
    result = result.reshape(NOCC, AUX, NVIR)
    return jnp.transpose(result, (1, 0, 2))
```

```python
import functools

import jax
import jax.numpy as jnp
from jax import lax
from jax.experimental import pallas as pl
from jax.experimental.pallas import tpu as pltpu
from jax.sharding import PartitionSpec as P

BLK = 64
OCC_DEV = 4
PARTNERS = 4
ROWS = 16
MIB = 1024 * 1024


def sort_kernel(orbitals, x_ref, mask_ref, out_ref):
    width = orbitals * ROWS
    block = x_ref.shape[0]
    row = lax.broadcasted_iota(jnp.int32, (width, width), 0)
    col = lax.broadcasted_iota(jnp.int32, (width, width), 1)
    hit = (row // ROWS == col % orbitals) & (row % ROWS == col // orbitals)
    for part in range(block // ROWS):
        spread = jnp.where(hit, mask_ref[part : part + 1, :], 0.0).astype(jnp.bfloat16)
        rows = x_ref[part * ROWS : (part + 1) * ROWS].reshape(width, x_ref.shape[2])
        moved = jnp.dot(spread, rows, preferred_element_type=jnp.float32).astype(jnp.bfloat16)
        out_ref[:, part * ROWS : (part + 1) * ROWS, :] = moved.reshape(orbitals, ROWS, -1)


def sorted_rows(half_ints, block_mask):
    rows, orbitals, basis = half_ints.shape
    block = 4 * ROWS
    width = orbitals * ROWS
    mask = jnp.repeat(block_mask, BLK // ROWS, axis=0).astype(jnp.float32)
    mask = jnp.tile(mask, (1, ROWS))
    steps = rows // block
    mask = mask.reshape(steps, block // ROWS, width)
    return pl.pallas_call(
        functools.partial(sort_kernel, orbitals),
        grid=(steps,),
        in_specs=[
            pl.BlockSpec((block, orbitals, basis), lambda g: (g, 0, 0)),
            pl.BlockSpec((None, block // ROWS, width), lambda g: (g, 0, 0)),
        ],
        out_specs=pl.BlockSpec((orbitals, block, basis), lambda g: (0, g, 0)),
        out_shape=jax.ShapeDtypeStruct((orbitals, rows, basis), jnp.bfloat16),
        compiler_params=pltpu.CompilerParams(vmem_limit_bytes=40 * MIB),
        cost_estimate=pl.CostEstimate(
            flops=2 * rows * orbitals * basis * width,
            bytes_accessed=4 * rows * orbitals * basis,
            transcendentals=0,
        ),
        name="sort_rows",
    )(half_ints, mask)


def transform_kernel(count, pos_ref, x_ref, dom_ref, coef_ref, *out_refs):
    step = pl.program_id(0)
    tile = 512
    whole = coef_ref.shape[1]
    dom = dom_ref[...]
    total = None
    for part in range(whole // tile):
        full = jnp.dot(
            x_ref[...], coef_ref[:, part * tile : (part + 1) * tile], preferred_element_type=jnp.float32
        ).astype(jnp.bfloat16)
        row = lax.broadcasted_iota(jnp.int32, (tile, dom.shape[1]), 0) + part * tile
        pick = jnp.where(row == dom, 1.0, 0.0).astype(jnp.bfloat16)
        term = jnp.dot(full, pick, preferred_element_type=jnp.float32)
        total = term if total is None else total + term
    total = total.astype(jnp.bfloat16)
    for index in range(count):
        @pl.when(step == index)
        def _():
            out_refs[index][...] = total


def transformed(rows_of, own_domains, vir_coef, aux_pos, chunk, count):
    orbitals, rows, basis = rows_of.shape
    virs = own_domains.shape[2]
    whole = vir_coef.shape[1]

    def orbital(step, pos_ref):
        return lax.rem(pos_ref[0] + step, count) * OCC_DEV + chunk

    return pl.pallas_call(
        functools.partial(transform_kernel, count),
        grid_spec=pltpu.PrefetchScalarGridSpec(
            num_scalar_prefetch=1,
            grid=(count,),
            in_specs=[
                pl.BlockSpec((None, rows, basis), lambda g, pos: (orbital(g, pos), 0, 0)),
                pl.BlockSpec((None, 1, virs), lambda g, pos: (orbital(g, pos), 0, 0)),
                pl.BlockSpec((basis, whole), lambda g, pos: (0, 0), pipeline_mode=pl.Buffered(1)),
            ],
            out_specs=[pl.BlockSpec((rows, virs), lambda g, pos: (0, 0)) for _ in range(count)],
        ),
        out_shape=[jax.ShapeDtypeStruct((rows, virs), jnp.bfloat16) for _ in range(count)],
        compiler_params=pltpu.CompilerParams(vmem_limit_bytes=40 * MIB),
        cost_estimate=pl.CostEstimate(
            flops=2 * count * rows * whole * (basis + virs),
            bytes_accessed=2 * (count * rows * (basis + virs) + basis * whole),
            transcendentals=0,
        ),
        name="transform",
    )(aux_pos, rows_of, own_domains, vir_coef)


def pair_kernel(chunk, count, live_ref, code_ref, odd_ref, occ_ref, own_ref, col_ref, row_ref, *refs):
    kinds = 5
    blocks = refs[: kinds * OCC_DEV]
    outs = refs[kinds * OCC_DEV : kinds * OCC_DEV + count]
    turned, total, held, sems, todo = refs[kinds * OCC_DEV + count :]
    span = PARTNERS * OCC_DEV
    slots = code_ref.shape[0]
    odd = odd_ref[0]

    def scan(slot, found):
        code = code_ref[slot]
        mine = (slot < live_ref[0]) & (code // span == chunk)

        @pl.when(mine)
        def _():
            todo[found] = code % span

        return found + mine.astype(jnp.int32)

    pairs = lax.fori_loop(0, slots, scan, jnp.int32(0))

    def source(slot):
        offset = slot // OCC_DEV
        one = jnp.where(odd == 1, 3, 1)
        three = jnp.where(odd == 1, 4, 3)
        kind = jnp.where(offset == 0, 0, jnp.where(offset == 1, one, jnp.where(offset == 2, 2, three)))
        return kind * OCC_DEV + slot % OCC_DEV

    def fetch(index):
        place = source(todo[index])
        buffer = lax.rem(index, 2)
        for number, block in enumerate(blocks):
            @pl.when(place == number)
            def _():
                pltpu.make_async_copy(block, held.at[buffer], sems.at[buffer]).start()

    @pl.when(pairs > 0)
    def _():
        fetch(0)
        turned[...] = own_ref[...].T

    total[...] = jnp.zeros_like(total)

    def step(index, carry):
        @pl.when(index + 1 < pairs)
        def _():
            fetch(index + 1)

        buffer = lax.rem(index, 2)
        pltpu.make_async_copy(blocks[0], held.at[buffer], sems.at[buffer]).wait()
        slot = todo[index]
        shift = occ_ref[chunk] + occ_ref[slot]
        other = held[buffer]
        exchange = jnp.dot(turned[...], other, preferred_element_type=jnp.float32)
        denom = (col_ref[...] + row_ref[slot]) - shift
        amplitude = (exchange / denom).astype(jnp.bfloat16)
        total[...] += lax.dot_general(
            other, amplitude, (((1,), (1,)), ((), ())), preferred_element_type=jnp.float32
        )
        return carry

    lax.fori_loop(0, pairs, step, jnp.int32(0))
    rows = outs[0].shape[0]
    for index, out in enumerate(outs):
        out[...] = total[index * rows : (index + 1) * rows, :].astype(jnp.bfloat16)


def densities(chunk, count, live, codes, odd, partner_occ, own, own_vir, vir_rows, blocks):
    aux, virs = own.shape
    rows = aux // count
    whole = lambda shape: pl.BlockSpec(shape, lambda: (0,) * len(shape))
    smem = pl.BlockSpec(memory_space=pltpu.SMEM)
    return pl.pallas_call(
        functools.partial(pair_kernel, chunk, count),
        in_specs=[smem, smem, smem, smem, whole(own.shape), whole(own_vir.shape), whole(vir_rows.shape)]
        + [pl.BlockSpec(memory_space=pl.ANY)] * len(blocks),
        out_specs=[whole((rows, virs))] * count,
        out_shape=[jax.ShapeDtypeStruct((rows, virs), jnp.bfloat16)] * count,
        scratch_shapes=[
            pltpu.VMEM((virs, aux), jnp.bfloat16),
            pltpu.VMEM((aux, virs), jnp.float32),
            pltpu.VMEM((2, aux, virs), jnp.bfloat16),
            pltpu.SemaphoreType.DMA((2,)),
            pltpu.SMEM((codes.shape[0],), jnp.int32),
        ],
        compiler_params=pltpu.CompilerParams(vmem_limit_bytes=40 * MIB),
        cost_estimate=pl.CostEstimate(
            flops=4 * 4 * aux * virs * virs, bytes_accessed=6 * aux * virs, transcendentals=0
        ),
        name="pairs",
    )(live, codes, odd, partner_occ, own, own_vir, vir_rows, *blocks)


def spread_kernel(count, pos_ref, *refs):
    pieces, out = refs[:-1], refs[-1]
    orbitals = count * OCC_DEV
    width = orbitals * ROWS
    row = lax.broadcasted_iota(jnp.int32, (width, width), 0)
    col = lax.broadcasted_iota(jnp.int32, (width, width), 1)
    group = col // ROWS
    place = lax.rem(pos_ref[0] + group % count, count) * OCC_DEV + group // count
    hit = jnp.where((row % orbitals == place) & (row // orbitals == col % ROWS), 1.0, 0.0).astype(jnp.bfloat16)
    for part in range(out.shape[0] // ROWS):
        span = pl.ds(part * ROWS, ROWS)
        rows = jnp.concatenate([piece[span, :] for piece in pieces], axis=0)
        moved = jnp.dot(hit, rows, preferred_element_type=jnp.float32).astype(jnp.bfloat16)
        out[span] = moved.reshape(ROWS, orbitals, -1)


def assembled(pieces, aux_pos, count):
    rows, virs = pieces[0].shape
    orbitals = count * OCC_DEV
    block = 4 * ROWS
    return pl.pallas_call(
        functools.partial(spread_kernel, count),
        grid_spec=pltpu.PrefetchScalarGridSpec(
            num_scalar_prefetch=1,
            grid=(rows // block,),
            in_specs=[pl.BlockSpec((block, virs), lambda g, pos: (g, 0))] * len(pieces),
            out_specs=pl.BlockSpec((block, orbitals, virs), lambda g, pos: (g, 0, 0)),
        ),
        out_shape=jax.ShapeDtypeStruct((rows, orbitals, virs), jnp.bfloat16),
        compiler_params=pltpu.CompilerParams(vmem_limit_bytes=40 * MIB),
        cost_estimate=pl.CostEstimate(
            flops=2 * rows * orbitals * virs * orbitals * ROWS,
            bytes_accessed=4 * rows * orbitals * virs,
            transcendentals=0,
        ),
        name="assemble",
    )(aux_pos, *pieces)


def body(half_ints, block_mask, vir_coef, domains, vir_energy, occ_energy, pair_count, pair_code):
    aux_count = lax.axis_size("aux")
    occ_count = lax.axis_size("occ")
    aux_pos = lax.axis_index("aux")
    occ_pos = lax.axis_index("occ")
    local_orbitals = half_ints.shape[1]
    pos = aux_pos.astype(jnp.int32).reshape(1)
    odd = (occ_pos % 2).astype(jnp.int32).reshape(1)

    def along_aux(value, steps):
        return lax.ppermute(value, "aux", [(z, (z + steps) % aux_count) for z in range(aux_count)])

    rows_of = sorted_rows(half_ints, block_mask)
    own_domains = lax.dynamic_slice_in_dim(domains, occ_pos * local_orbitals, local_orbitals, 0)
    own_domains = own_domains[:, None, :]

    dom_rows = []
    occ_rows = []
    for offset in range(PARTNERS):
        start = ((occ_pos + offset) % occ_count * aux_count + aux_pos) * OCC_DEV
        dom_rows.append(lax.dynamic_slice_in_dim(domains, start, OCC_DEV, 0))
        occ_rows.append(lax.dynamic_slice_in_dim(occ_energy, start, OCC_DEV, 0))
    partner_vir = jnp.take(vir_energy, jnp.concatenate(dom_rows, axis=0))
    partner_occ = jnp.concatenate(occ_rows, axis=0)

    twin = [(n, n ^ 1) for n in range(occ_count)]
    next_chip = [(n, (n - 2) % occ_count) for n in range(occ_count)]
    third = [((n + 3) % occ_count, n) for n in range(1, occ_count, 2)]
    own, swap, chip, cross, far = [], [], [], [], []
    for chunk in range(OCC_DEV):
        pieces = transformed(rows_of, own_domains, vir_coef, pos, chunk, aux_count)
        pieces = [pieces[0]] + [along_aux(pieces[step], step) for step in range(1, aux_count)]
        orbital = jnp.concatenate(pieces, axis=0)
        own.append(orbital)
        swap.append(lax.ppermute(orbital, "occ", twin))
        chip.append(lax.ppermute(orbital, "occ", next_chip))
        cross.append(lax.ppermute(chip[-1], "occ", twin))
        far.append(lax.ppermute(orbital, "occ", third))
    blocks = own + swap + chip + cross + far
    live = pair_count[0]
    codes = pair_code[0, 0]
    results = []
    for chunk in range(OCC_DEV):
        pieces = densities(
            chunk, aux_count, live, codes, odd, partner_occ, own[chunk],
            partner_vir[chunk][:, None], partner_vir[:, None, :], blocks,
        )
        results += [pieces[0]] + [along_aux(pieces[step], -step) for step in range(1, aux_count)]
    return assembled(results, pos, aux_count)


def solution(mesh):
    placed = (
        P("aux", "occ", None),
        P("aux", "occ"),
        P(),
        P(),
        P(),
        P(),
        P("occ", "aux"),
        P("occ", "aux", None),
    )
    return jax.shard_map(
        body, mesh=mesh, in_specs=placed, out_specs=P("aux", "occ", None), check_vma=False
    )
```

```python
import functools

import jax
import jax.numpy as jnp
from jax import lax
from jax.experimental import pallas as pl
from jax.experimental.pallas import tpu as pltpu
from jax.sharding import PartitionSpec as P

BLK = 64
OCC_DEV = 4
PARTNERS = 4
ROWS = 16
MIB = 1024 * 1024


def sort_kernel(orbitals, x_ref, mask_ref, out_ref):
    width = orbitals * ROWS
    block = x_ref.shape[0]
    row = lax.broadcasted_iota(jnp.int32, (width, width), 0)
    col = lax.broadcasted_iota(jnp.int32, (width, width), 1)
    hit = (row // ROWS == col % orbitals) & (row % ROWS == col // orbitals)
    for part in range(block // ROWS):
        spread = jnp.where(hit, mask_ref[part : part + 1, :], 0.0).astype(jnp.bfloat16)
        rows = x_ref[part * ROWS : (part + 1) * ROWS].reshape(width, x_ref.shape[2])
        moved = jnp.dot(spread, rows, preferred_element_type=jnp.float32).astype(jnp.bfloat16)
        out_ref[:, part * ROWS : (part + 1) * ROWS, :] = moved.reshape(orbitals, ROWS, -1)


def sorted_rows(half_ints, block_mask):
    rows, orbitals, basis = half_ints.shape
    block = 4 * ROWS
    width = orbitals * ROWS
    mask = jnp.repeat(block_mask, BLK // ROWS, axis=0).astype(jnp.float32)
    mask = jnp.tile(mask, (1, ROWS))
    steps = rows // block
    mask = mask.reshape(steps, block // ROWS, width)
    return pl.pallas_call(
        functools.partial(sort_kernel, orbitals),
        grid=(steps,),
        in_specs=[
            pl.BlockSpec((block, orbitals, basis), lambda g: (g, 0, 0)),
            pl.BlockSpec((None, block // ROWS, width), lambda g: (g, 0, 0)),
        ],
        out_specs=pl.BlockSpec((orbitals, block, basis), lambda g: (0, g, 0)),
        out_shape=jax.ShapeDtypeStruct((orbitals, rows, basis), jnp.bfloat16),
        compiler_params=pltpu.CompilerParams(vmem_limit_bytes=40 * MIB),
        cost_estimate=pl.CostEstimate(
            flops=2 * rows * orbitals * basis * width,
            bytes_accessed=4 * rows * orbitals * basis,
            transcendentals=0,
        ),
        name="sort_rows",
    )(half_ints, mask)


def transform_kernel(count, after, pos_ref, x_ref, dom_ref, coef_ref, *refs):
    out_refs = refs[after:]
    step = pl.program_id(0)
    tile = 512
    whole = coef_ref.shape[1]
    dom = dom_ref[...]
    total = None
    for part in range(whole // tile):
        full = jnp.dot(
            x_ref[...], coef_ref[:, part * tile : (part + 1) * tile], preferred_element_type=jnp.float32
        ).astype(jnp.bfloat16)
        row = lax.broadcasted_iota(jnp.int32, (tile, dom.shape[1]), 0) + part * tile
        pick = jnp.where(row == dom, 1.0, 0.0).astype(jnp.bfloat16)
        term = jnp.dot(full, pick, preferred_element_type=jnp.float32)
        total = term if total is None else total + term
    total = total.astype(jnp.bfloat16)
    for index in range(count):
        @pl.when(step == index)
        def _():
            out_refs[index][...] = total


def transformed(rows_of, own_domains, vir_coef, aux_pos, aux_count, chunk, first, count, after):
    orbitals, rows, basis = rows_of.shape
    virs = own_domains.shape[2]
    whole = vir_coef.shape[1]

    def orbital(step, pos_ref):
        return lax.rem(pos_ref[0] + first + step, aux_count) * OCC_DEV + chunk

    return pl.pallas_call(
        functools.partial(transform_kernel, count, len(after)),
        grid_spec=pltpu.PrefetchScalarGridSpec(
            num_scalar_prefetch=1,
            grid=(count,),
            in_specs=[
                pl.BlockSpec((None, rows, basis), lambda g, pos: (orbital(g, pos), 0, 0)),
                pl.BlockSpec((None, 1, virs), lambda g, pos: (orbital(g, pos), 0, 0)),
                pl.BlockSpec((basis, whole), lambda g, pos: (0, 0), pipeline_mode=pl.Buffered(1)),
            ]
            + [pl.BlockSpec(memory_space=pl.ANY)] * len(after),
            out_specs=[pl.BlockSpec((rows, virs), lambda g, pos: (0, 0)) for _ in range(count)],
        ),
        out_shape=[jax.ShapeDtypeStruct((rows, virs), jnp.bfloat16) for _ in range(count)],
        compiler_params=pltpu.CompilerParams(vmem_limit_bytes=40 * MIB),
        cost_estimate=pl.CostEstimate(
            flops=2 * count * rows * whole * (basis + virs),
            bytes_accessed=2 * (count * rows * (basis + virs) + basis * whole),
            transcendentals=0,
        ),
        name="transform",
    )(aux_pos, rows_of, own_domains, vir_coef, *after)


def join_kernel(count, after, flag_ref, *refs):
    pieces, out, sems = refs[:count], refs[count + after], refs[count + after + 1]
    rows = pieces[0].shape[0]
    copies = [
        pltpu.make_async_copy(piece, out.at[pl.ds(index * rows, rows)], sems.at[index])
        for index, piece in enumerate(pieces)
    ]
    for copy in copies:
        copy.start()
    for copy in copies:
        copy.wait()


def pick_kernel(flag_ref, own_ref, near_ref, late_ref, *refs):
    out, sems = refs[-2:]
    rows = own_ref.shape[0]
    first = pltpu.make_async_copy(own_ref, out.at[pl.ds(0, rows)], sems.at[0])
    near = pltpu.make_async_copy(near_ref, out.at[pl.ds(rows, rows)], sems.at[1])
    late = pltpu.make_async_copy(late_ref, out.at[pl.ds(rows, rows)], sems.at[1])
    first.start()

    @pl.when(flag_ref[0] == 0)
    def _():
        near.start()

    @pl.when(flag_ref[0] != 0)
    def _():
        late.start()

    first.wait()
    near.wait()


def stacked(pieces, flag, after):
    rows = sum(piece.shape[0] for piece in pieces)
    held = pl.BlockSpec(memory_space=pl.ANY)
    return pl.pallas_call(
        functools.partial(join_kernel, len(pieces), len(after)),
        in_specs=[pl.BlockSpec(memory_space=pltpu.SMEM)] + [held] * (len(pieces) + len(after)),
        out_specs=held,
        out_shape=jax.ShapeDtypeStruct((rows,) + pieces[0].shape[1:], pieces[0].dtype),
        scratch_shapes=[pltpu.SemaphoreType.DMA((len(pieces),))],
        cost_estimate=pl.CostEstimate(
            flops=0, bytes_accessed=4 * rows * pieces[0].shape[1], transcendentals=0
        ),
        name="join",
    )(flag, *pieces, *after)


def with_next(own, near, late, flag, after):
    rows = own.shape[0]
    held = pl.BlockSpec(memory_space=pl.ANY)
    return pl.pallas_call(
        pick_kernel,
        in_specs=[pl.BlockSpec(memory_space=pltpu.SMEM)] + [held] * (3 + len(after)),
        out_specs=held,
        out_shape=jax.ShapeDtypeStruct((2 * rows,) + own.shape[1:], own.dtype),
        scratch_shapes=[pltpu.SemaphoreType.DMA((2,))],
        cost_estimate=pl.CostEstimate(flops=0, bytes_accessed=8 * rows * own.shape[1], transcendentals=0),
        name="pick",
    )(flag, own, near, late, *after)


def energy_kernel(dom_ref, table_ref, row_ref, col_ref):
    slots, virs = dom_ref.shape
    lanes = table_ref.shape[1]
    for part in range(virs // lanes):
        span = slice(part * lanes, (part + 1) * lanes)
        dom = dom_ref[:, span]
        high, low = dom // lanes, dom % lanes
        total = jnp.zeros((slots, lanes), jnp.float32)
        for line in range(table_ref.shape[0]):
            table = jnp.broadcast_to(table_ref[line : line + 1, :], (slots, lanes))
            found = jnp.take_along_axis(table, low, axis=1, mode="promise_in_bounds")
            total = jnp.where(high == line, found, total)
        row_ref[:, 0, span] = total
        col_ref[span, :] = total.T


def energies(dom, vir_energy):
    slots, virs = dom.shape
    return pl.pallas_call(
        energy_kernel,
        out_shape=[
            jax.ShapeDtypeStruct((slots, 1, virs), jnp.float32),
            jax.ShapeDtypeStruct((virs, slots), jnp.float32),
        ],
        name="energies",
    )(dom, vir_energy.reshape(-1, 128))


def pair_kernel(chunk, count, live_ref, code_ref, odd_ref, occ_ref, own_ref, col_ref, row_ref, *refs):
    sets = 3
    rows = own_ref.shape[0]
    blocks = refs[: sets * OCC_DEV]
    outs = refs[sets * OCC_DEV : sets * OCC_DEV + count]
    turned, total, held, sems, todo = refs[sets * OCC_DEV + count :]
    span = PARTNERS * OCC_DEV
    slots = code_ref.shape[0]
    odd = odd_ref[0]

    def scan(slot, found):
        code = code_ref[slot]
        mine = (slot < live_ref[0]) & (code // span == chunk)

        @pl.when(mine)
        def _():
            todo[found] = code % span

        return found + mine.astype(jnp.int32)

    pairs = lax.fori_loop(0, slots, scan, jnp.int32(0))

    def source(slot):
        offset = slot // OCC_DEV
        one = jnp.where(odd == 1, 3, 2)
        three = jnp.where(odd == 1, 4, 3)
        kind = jnp.where(offset == 0, 0, jnp.where(offset == 1, one, jnp.where(offset == 2, 1, three)))
        return kind * OCC_DEV + slot % OCC_DEV

    def fetch(index):
        place = source(todo[index])
        buffer = lax.rem(index, 2)
        for kind in range(5):
            for orbital in range(OCC_DEV):
                block = blocks[kind // 2 * OCC_DEV + orbital].at[pl.ds(kind % 2 * rows, rows)]

                @pl.when(place == kind * OCC_DEV + orbital)
                def _():
                    pltpu.make_async_copy(block, held.at[buffer], sems.at[buffer]).start()

    @pl.when(pairs > 0)
    def _():
        fetch(0)
        turned[...] = own_ref[...].T

    total[...] = jnp.zeros_like(total)

    def step(index, carry):
        @pl.when(index + 1 < pairs)
        def _():
            fetch(index + 1)

        buffer = lax.rem(index, 2)
        pltpu.make_async_copy(blocks[0].at[pl.ds(0, rows)], held.at[buffer], sems.at[buffer]).wait()
        slot = todo[index]
        shift = occ_ref[chunk] + occ_ref[slot]
        other = held[buffer]
        exchange = jnp.dot(turned[...], other, preferred_element_type=jnp.float32)
        denom = (col_ref[:, chunk : chunk + 1] + row_ref[slot]) - shift
        amplitude = (exchange / denom).astype(jnp.bfloat16)
        total[...] += lax.dot_general(
            other, amplitude, (((1,), (1,)), ((), ())), preferred_element_type=jnp.float32
        )
        return carry

    lax.fori_loop(0, pairs, step, jnp.int32(0))
    part = outs[0].shape[0]
    for index, out in enumerate(outs):
        out[...] = total[index * part : (index + 1) * part, :].astype(jnp.bfloat16)


def densities(chunk, count, live, codes, odd, partner_occ, own, own_vir, vir_rows, blocks):
    aux, virs = own.shape
    rows = aux // count
    whole = lambda shape: pl.BlockSpec(shape, lambda: (0,) * len(shape))
    smem = pl.BlockSpec(memory_space=pltpu.SMEM)
    return pl.pallas_call(
        functools.partial(pair_kernel, chunk, count),
        in_specs=[smem, smem, smem, smem, whole(own.shape), whole(own_vir.shape), whole(vir_rows.shape)]
        + [pl.BlockSpec(memory_space=pltpu.HBM)] * len(blocks),
        out_specs=[whole((rows, virs))] * count,
        out_shape=[jax.ShapeDtypeStruct((rows, virs), jnp.bfloat16)] * count,
        scratch_shapes=[
            pltpu.VMEM((virs, aux), jnp.bfloat16),
            pltpu.VMEM((aux, virs), jnp.float32),
            pltpu.VMEM((2, aux, virs), jnp.bfloat16),
            pltpu.SemaphoreType.DMA((2,)),
            pltpu.SMEM((codes.shape[0],), jnp.int32),
        ],
        compiler_params=pltpu.CompilerParams(vmem_limit_bytes=40 * MIB),
        cost_estimate=pl.CostEstimate(
            flops=4 * 4 * aux * virs * virs, bytes_accessed=6 * aux * virs, transcendentals=0
        ),
        name="pairs",
    )(live, codes, odd, partner_occ, own, own_vir, vir_rows, *blocks)


def spread_kernel(count, pos_ref, *refs):
    pieces, out = refs[:-1], refs[-1]
    orbitals = count * OCC_DEV
    width = orbitals * ROWS
    row = lax.broadcasted_iota(jnp.int32, (width, width), 0)
    col = lax.broadcasted_iota(jnp.int32, (width, width), 1)
    group = col // ROWS
    place = lax.rem(pos_ref[0] + group % count, count) * OCC_DEV + group // count
    hit = jnp.where((row % orbitals == place) & (row // orbitals == col % ROWS), 1.0, 0.0).astype(jnp.bfloat16)
    for part in range(out.shape[0] // ROWS):
        span = pl.ds(part * ROWS, ROWS)
        rows = jnp.concatenate([piece[span, :] for piece in pieces], axis=0)
        moved = jnp.dot(hit, rows, preferred_element_type=jnp.float32).astype(jnp.bfloat16)
        out[span] = moved.reshape(ROWS, orbitals, -1)


def assembled(pieces, aux_pos, count):
    rows, virs = pieces[0].shape
    orbitals = count * OCC_DEV
    block = 4 * ROWS
    return pl.pallas_call(
        functools.partial(spread_kernel, count),
        grid_spec=pltpu.PrefetchScalarGridSpec(
            num_scalar_prefetch=1,
            grid=(rows // block,),
            in_specs=[pl.BlockSpec((block, virs), lambda g, pos: (g, 0))] * len(pieces),
            out_specs=pl.BlockSpec((block, orbitals, virs), lambda g, pos: (g, 0, 0)),
        ),
        out_shape=jax.ShapeDtypeStruct((rows, orbitals, virs), jnp.bfloat16),
        compiler_params=pltpu.CompilerParams(vmem_limit_bytes=40 * MIB),
        cost_estimate=pl.CostEstimate(
            flops=2 * rows * orbitals * virs * orbitals * ROWS,
            bytes_accessed=4 * rows * orbitals * virs,
            transcendentals=0,
        ),
        name="assemble",
    )(aux_pos, *pieces)


def body(half_ints, block_mask, vir_coef, domains, vir_energy, occ_energy, pair_count, pair_code):
    aux_count = lax.axis_size("aux")
    occ_count = lax.axis_size("occ")
    aux_pos = lax.axis_index("aux")
    occ_pos = lax.axis_index("occ")
    local_orbitals = half_ints.shape[1]
    pos = aux_pos.astype(jnp.int32).reshape(1)
    odd = (occ_pos % 2).astype(jnp.int32).reshape(1)

    def along_aux(value, steps):
        return lax.ppermute(value, "aux", [(z, (z + steps) % aux_count) for z in range(aux_count)])

    rows_of = sorted_rows(half_ints, block_mask)
    own_domains = lax.dynamic_slice_in_dim(domains, occ_pos * local_orbitals, local_orbitals, 0)
    own_domains = own_domains[:, None, :]

    dom_rows = []
    occ_rows = []
    for offset in range(PARTNERS):
        start = ((occ_pos + offset) % occ_count * aux_count + aux_pos) * OCC_DEV
        dom_rows.append(lax.dynamic_slice_in_dim(domains, start, OCC_DEV, 0))
        occ_rows.append(lax.dynamic_slice_in_dim(occ_energy, start, OCC_DEV, 0))
    vir_rows, vir_cols = energies(jnp.concatenate(dom_rows, axis=0), vir_energy)
    partner_occ = jnp.concatenate(occ_rows, axis=0)

    twin, direct, far, last, late = routes(occ_count)
    is_late = functools.reduce(jnp.logical_or, [occ_pos == n for n in late], jnp.bool_(False))
    is_late = is_late.astype(jnp.int32).reshape(1)
    owns, nears, sets, swaps, thirds = [], [], [], [], []
    transform = functools.partial(transformed, rows_of, own_domains, vir_coef, pos, aux_count)
    sent = [None] * aux_count
    for step in list(range(1, aux_count)) + [0]:
        sent[step] = transform(0, step, 1, [])[0]
    after = [sent[0], vir_rows, partner_occ]
    pieces = [sent[0]] + [along_aux(sent[step], step) for step in range(1, aux_count)]
    for chunk in range(OCC_DEV):
        coming = []
        if chunk + 1 < OCC_DEV:
            sent = transform(chunk + 1, 0, aux_count, after)
            coming = [sent[0]] + [along_aux(sent[step], step) for step in range(1, aux_count)]
        own = stacked(pieces, is_late, nears[-1:] + thirds[-1:] + swaps[-2:-1] + coming[:1])
        near = lax.ppermute(own, "occ", direct)
        third = lax.ppermute(own, "occ", far)
        late_near = lax.ppermute(third, "occ", last) if last else near
        both = with_next(own, near, late_near, is_late, coming[1:])
        swap = lax.ppermute(both, "occ", twin)
        for kind, value in zip((owns, nears, sets, swaps, thirds), (own, near, both, swap, third)):
            kind.append(value)
        pieces, after = coming, [own]
    blocks = sets + swaps + thirds
    live = pair_count[0]
    codes = pair_code[0, 0]
    results = []
    for chunk in range(OCC_DEV):
        pieces = densities(
            chunk, aux_count, live, codes, odd, partner_occ, owns[chunk], vir_cols, vir_rows, blocks
        )
        results += [pieces[0]] + [along_aux(pieces[step], -step) for step in range(1, aux_count)]
    return assembled(results, pos, aux_count)


def routes(count):
    chips = count // 2
    twin = [(n, n ^ 1) for n in range(count)]
    turned = [c for c in range(0, chips, 2)] if chips == 4 else []
    direct = [(n, (n - 2) % count) for n in range(count) if not (n % 2 and n // 2 in turned)]
    far = [((n + 3) % count, n) for n in range(1, count, 2)]
    far += [(2 * c + 1, 2 * ((c + 2) % chips)) for c in turned]
    last = [(2 * ((c + 2) % chips), 2 * ((c - 1) % chips) + 1) for c in turned]
    late = [target for _, target in last]
    return twin, direct, far, last, late


def solution(mesh):
    placed = (
        P("aux", "occ", None),
        P("aux", "occ"),
        P(),
        P(),
        P(),
        P(),
        P("occ", "aux"),
        P("occ", "aux", None),
    )
    return jax.shard_map(
        body, mesh=mesh, in_specs=placed, out_specs=P("aux", "occ", None), check_vma=False
    )
```

```python
import functools

import jax
import jax.numpy as jnp
from jax import lax
from jax.experimental import pallas as pl
from jax.experimental.pallas import tpu as pltpu
from jax.sharding import PartitionSpec as P

BLK = 64
OCC_DEV = 4
PARTNERS = 4
ROWS = 16
MIB = 1024 * 1024


def sort_kernel(orbitals, x_ref, mask_ref, out_ref):
    width = orbitals * ROWS
    block = x_ref.shape[0]
    row = lax.broadcasted_iota(jnp.int32, (width, width), 0)
    col = lax.broadcasted_iota(jnp.int32, (width, width), 1)
    hit = (row // ROWS == col % orbitals) & (row % ROWS == col // orbitals)
    for part in range(block // ROWS):
        spread = jnp.where(hit, mask_ref[part : part + 1, :], 0.0).astype(jnp.bfloat16)
        rows = x_ref[part * ROWS : (part + 1) * ROWS].reshape(width, x_ref.shape[2])
        moved = jnp.dot(spread, rows, preferred_element_type=jnp.float32).astype(jnp.bfloat16)
        out_ref[:, part * ROWS : (part + 1) * ROWS, :] = moved.reshape(orbitals, ROWS, -1)


def sorted_rows(half_ints, block_mask):
    rows, orbitals, basis = half_ints.shape
    block = 4 * ROWS
    width = orbitals * ROWS
    mask = jnp.repeat(block_mask, BLK // ROWS, axis=0).astype(jnp.float32)
    mask = jnp.tile(mask, (1, ROWS))
    steps = rows // block
    mask = mask.reshape(steps, block // ROWS, width)
    return pl.pallas_call(
        functools.partial(sort_kernel, orbitals),
        grid=(steps,),
        in_specs=[
            pl.BlockSpec((block, orbitals, basis), lambda g: (g, 0, 0)),
            pl.BlockSpec((None, block // ROWS, width), lambda g: (g, 0, 0)),
        ],
        out_specs=pl.BlockSpec((orbitals, block, basis), lambda g: (0, g, 0)),
        out_shape=jax.ShapeDtypeStruct((orbitals, rows, basis), jnp.bfloat16),
        compiler_params=pltpu.CompilerParams(vmem_limit_bytes=24 * MIB),
        cost_estimate=pl.CostEstimate(
            flops=2 * rows * orbitals * basis * width,
            bytes_accessed=4 * rows * orbitals * basis,
            transcendentals=0,
        ),
        name="sort_rows",
    )(half_ints, mask)


def transform_kernel(count, after, pos_ref, x_ref, dom_ref, coef_ref, *refs):
    out_refs = refs[after:]
    step = pl.program_id(0)
    tile = 512
    whole = coef_ref.shape[1]
    dom = dom_ref[...]
    total = None
    for part in range(whole // tile):
        full = jnp.dot(
            x_ref[...], coef_ref[:, part * tile : (part + 1) * tile], preferred_element_type=jnp.float32
        ).astype(jnp.bfloat16)
        row = lax.broadcasted_iota(jnp.int32, (tile, dom.shape[1]), 0) + part * tile
        pick = jnp.where(row == dom, 1.0, 0.0).astype(jnp.bfloat16)
        term = jnp.dot(full, pick, preferred_element_type=jnp.float32)
        total = term if total is None else total + term
    total = total.astype(jnp.bfloat16)
    for index in range(count):
        @pl.when(step == index)
        def _():
            out_refs[index][...] = total


def transformed(rows_of, own_domains, vir_coef, aux_pos, aux_count, chunk, first, count, after):
    orbitals, rows, basis = rows_of.shape
    virs = own_domains.shape[2]
    whole = vir_coef.shape[1]

    def orbital(step, pos_ref):
        return lax.rem(pos_ref[0] + first + step, aux_count) * OCC_DEV + chunk

    return pl.pallas_call(
        functools.partial(transform_kernel, count, len(after)),
        grid_spec=pltpu.PrefetchScalarGridSpec(
            num_scalar_prefetch=1,
            grid=(count,),
            in_specs=[
                pl.BlockSpec((None, rows, basis), lambda g, pos: (orbital(g, pos), 0, 0)),
                pl.BlockSpec((None, 1, virs), lambda g, pos: (orbital(g, pos), 0, 0)),
                pl.BlockSpec((basis, whole), lambda g, pos: (0, 0), pipeline_mode=pl.Buffered(1)),
            ]
            + [pl.BlockSpec(memory_space=pl.ANY)] * len(after),
            out_specs=[pl.BlockSpec((rows, virs), lambda g, pos: (0, 0)) for _ in range(count)],
        ),
        out_shape=[jax.ShapeDtypeStruct((rows, virs), jnp.bfloat16) for _ in range(count)],
        compiler_params=pltpu.CompilerParams(vmem_limit_bytes=20 * MIB),
        cost_estimate=pl.CostEstimate(
            flops=2 * count * rows * whole * (basis + virs),
            bytes_accessed=2 * (count * rows * (basis + virs) + basis * whole),
            transcendentals=0,
        ),
        name="transform",
    )(aux_pos, rows_of, own_domains, vir_coef, *after)


def join_kernel(count, *refs):
    out = refs[-1]
    rows = refs[0].shape[0]
    for index in range(count):
        out[index * rows : (index + 1) * rows, :] = refs[index][...]


def stacked(pieces, after):
    rows, virs = pieces[0].shape
    count = len(pieces)
    return pl.pallas_call(
        functools.partial(join_kernel, count),
        in_specs=[pl.BlockSpec((rows, virs), lambda: (0, 0))] * count
        + [pl.BlockSpec(memory_space=pl.ANY)] * len(after),
        out_specs=pl.BlockSpec((count * rows, virs), lambda: (0, 0)),
        out_shape=jax.ShapeDtypeStruct((count * rows, virs), pieces[0].dtype),
        compiler_params=pltpu.CompilerParams(vmem_limit_bytes=16 * MIB),
        cost_estimate=pl.CostEstimate(flops=0, bytes_accessed=4 * count * rows * virs, transcendentals=0),
        name="join",
    )(*pieces, *after)


def pick_kernel(flag_ref, own_ref, near_ref, late_ref, *refs):
    out = refs[-1]
    out[0] = own_ref[...]

    @pl.when(flag_ref[0] == 0)
    def _():
        out[1] = near_ref[...]

    @pl.when(flag_ref[0] != 0)
    def _():
        out[1] = late_ref[...]


def with_next(own, near, late, flag, after):
    rows, virs = own.shape
    block = rows // 4
    return pl.pallas_call(
        pick_kernel,
        grid=(rows // block,),
        in_specs=[pl.BlockSpec(memory_space=pltpu.SMEM)]
        + [pl.BlockSpec((block, virs), lambda g: (g, 0))] * 3
        + [pl.BlockSpec(memory_space=pl.ANY)] * len(after),
        out_specs=pl.BlockSpec((2, block, virs), lambda g: (0, g, 0)),
        out_shape=jax.ShapeDtypeStruct((2, rows, virs), own.dtype),
        compiler_params=pltpu.CompilerParams(vmem_limit_bytes=16 * MIB),
        cost_estimate=pl.CostEstimate(flops=0, bytes_accessed=10 * rows * virs, transcendentals=0),
        name="pick",
    )(flag, own, near, late, *after)


def energy_kernel(dom_ref, table_ref, row_ref, col_ref):
    slots, virs = dom_ref.shape
    lanes = table_ref.shape[1]
    for part in range(virs // lanes):
        span = slice(part * lanes, (part + 1) * lanes)
        dom = dom_ref[:, span]
        high, low = dom // lanes, dom % lanes
        total = jnp.zeros((slots, lanes), jnp.float32)
        for line in range(table_ref.shape[0]):
            table = jnp.broadcast_to(table_ref[line : line + 1, :], (slots, lanes))
            found = jnp.take_along_axis(table, low, axis=1, mode="promise_in_bounds")
            total = jnp.where(high == line, found, total)
        row_ref[:, 0, span] = total
        col_ref[span, :] = total.T


def energies(dom, vir_energy):
    slots, virs = dom.shape
    return pl.pallas_call(
        energy_kernel,
        out_shape=[
            jax.ShapeDtypeStruct((slots, 1, virs), jnp.float32),
            jax.ShapeDtypeStruct((virs, slots), jnp.float32),
        ],
        name="energies",
    )(dom, vir_energy.reshape(-1, 128))


def pair_kernel(chunk, count, live_ref, code_ref, odd_ref, occ_ref, own_ref, col_ref, row_ref, *refs):
    sets = 3
    blocks = refs[: sets * OCC_DEV]
    outs = refs[sets * OCC_DEV : sets * OCC_DEV + count]
    turned, total, held, sems, todo = refs[sets * OCC_DEV + count :]
    span = PARTNERS * OCC_DEV
    slots = code_ref.shape[0]
    odd = odd_ref[0]

    def scan(slot, found):
        code = code_ref[slot]
        mine = (slot < live_ref[0]) & (code // span == chunk)

        @pl.when(mine)
        def _():
            todo[found] = code % span

        return found + mine.astype(jnp.int32)

    pairs = lax.fori_loop(0, slots, scan, jnp.int32(0))

    def source(slot):
        offset = slot // OCC_DEV
        one = jnp.where(odd == 1, 3, 2)
        three = jnp.where(odd == 1, 4, 3)
        kind = jnp.where(offset == 0, 0, jnp.where(offset == 1, one, jnp.where(offset == 2, 1, three)))
        return kind * OCC_DEV + slot % OCC_DEV

    def fetch(index):
        place = source(todo[index])
        buffer = lax.rem(index, 2)
        for kind in range(5):
            for orbital in range(OCC_DEV):
                block = blocks[kind // 2 * OCC_DEV + orbital]
                block = block.at[kind % 2] if kind < 4 else block

                @pl.when(place == kind * OCC_DEV + orbital)
                def _():
                    pltpu.make_async_copy(block, held.at[buffer], sems.at[buffer]).start()

    @pl.when(pairs > 0)
    def _():
        fetch(0)
        turned[...] = own_ref[...].T

    total[...] = jnp.zeros_like(total)

    def step(index, carry):
        @pl.when(index + 1 < pairs)
        def _():
            fetch(index + 1)

        buffer = lax.rem(index, 2)
        pltpu.make_async_copy(blocks[0].at[0], held.at[buffer], sems.at[buffer]).wait()
        slot = todo[index]
        shift = occ_ref[chunk] + occ_ref[slot]
        other = held[buffer]
        exchange = jnp.dot(turned[...], other, preferred_element_type=jnp.float32)
        denom = (col_ref[:, chunk : chunk + 1] + row_ref[slot]) - shift
        amplitude = (exchange / denom).astype(jnp.bfloat16)
        total[...] += lax.dot_general(
            other, amplitude, (((1,), (1,)), ((), ())), preferred_element_type=jnp.float32
        )
        return carry

    lax.fori_loop(0, pairs, step, jnp.int32(0))
    part = outs[0].shape[0]
    for index, out in enumerate(outs):
        out[...] = total[index * part : (index + 1) * part, :].astype(jnp.bfloat16)


def densities(chunk, count, live, codes, odd, partner_occ, own, own_vir, vir_rows, blocks):
    aux, virs = own.shape
    rows = aux // count
    whole = lambda shape: pl.BlockSpec(shape, lambda: (0,) * len(shape))
    smem = pl.BlockSpec(memory_space=pltpu.SMEM)
    return pl.pallas_call(
        functools.partial(pair_kernel, chunk, count),
        in_specs=[smem, smem, smem, smem, whole(own.shape), whole(own_vir.shape), whole(vir_rows.shape)]
        + [pl.BlockSpec(memory_space=pltpu.HBM)] * len(blocks),
        out_specs=[whole((rows, virs))] * count,
        out_shape=[jax.ShapeDtypeStruct((rows, virs), jnp.bfloat16)] * count,
        scratch_shapes=[
            pltpu.VMEM((virs, aux), jnp.bfloat16),
            pltpu.VMEM((aux, virs), jnp.float32),
            pltpu.VMEM((2, aux, virs), jnp.bfloat16),
            pltpu.SemaphoreType.DMA((2,)),
            pltpu.SMEM((codes.shape[0],), jnp.int32),
        ],
        compiler_params=pltpu.CompilerParams(vmem_limit_bytes=40 * MIB),
        cost_estimate=pl.CostEstimate(
            flops=4 * 4 * aux * virs * virs, bytes_accessed=6 * aux * virs, transcendentals=0
        ),
        name="pairs",
    )(live, codes, odd, partner_occ, own, own_vir, vir_rows, *blocks)


def spread_kernel(count, pos_ref, *refs):
    pieces, out = refs[:-1], refs[-1]
    orbitals = count * OCC_DEV
    width = orbitals * ROWS
    row = lax.broadcasted_iota(jnp.int32, (width, width), 0)
    col = lax.broadcasted_iota(jnp.int32, (width, width), 1)
    group = col // ROWS
    place = lax.rem(pos_ref[0] + group % count, count) * OCC_DEV + group // count
    hit = jnp.where((row % orbitals == place) & (row // orbitals == col % ROWS), 1.0, 0.0).astype(jnp.bfloat16)
    for part in range(out.shape[0] // ROWS):
        span = pl.ds(part * ROWS, ROWS)
        rows = jnp.concatenate([piece[span, :] for piece in pieces], axis=0)
        moved = jnp.dot(hit, rows, preferred_element_type=jnp.float32).astype(jnp.bfloat16)
        out[span] = moved.reshape(ROWS, orbitals, -1)


def assembled(pieces, aux_pos, count):
    rows, virs = pieces[0].shape
    orbitals = count * OCC_DEV
    block = 4 * ROWS
    return pl.pallas_call(
        functools.partial(spread_kernel, count),
        grid_spec=pltpu.PrefetchScalarGridSpec(
            num_scalar_prefetch=1,
            grid=(rows // block,),
            in_specs=[pl.BlockSpec((block, virs), lambda g, pos: (g, 0))] * len(pieces),
            out_specs=pl.BlockSpec((block, orbitals, virs), lambda g, pos: (g, 0, 0)),
        ),
        out_shape=jax.ShapeDtypeStruct((rows, orbitals, virs), jnp.bfloat16),
        compiler_params=pltpu.CompilerParams(vmem_limit_bytes=40 * MIB),
        cost_estimate=pl.CostEstimate(
            flops=2 * rows * orbitals * virs * orbitals * ROWS,
            bytes_accessed=4 * rows * orbitals * virs,
            transcendentals=0,
        ),
        name="assemble",
    )(aux_pos, *pieces)


def body(half_ints, block_mask, vir_coef, domains, vir_energy, occ_energy, pair_count, pair_code):
    aux_count = lax.axis_size("aux")
    occ_count = lax.axis_size("occ")
    aux_pos = lax.axis_index("aux")
    occ_pos = lax.axis_index("occ")
    local_orbitals = half_ints.shape[1]
    pos = aux_pos.astype(jnp.int32).reshape(1)
    odd = (occ_pos % 2).astype(jnp.int32).reshape(1)

    def along_aux(value, steps):
        return lax.ppermute(value, "aux", [(z, (z + steps) % aux_count) for z in range(aux_count)])

    rows_of = sorted_rows(half_ints, block_mask)
    own_domains = lax.dynamic_slice_in_dim(domains, occ_pos * local_orbitals, local_orbitals, 0)
    own_domains = own_domains[:, None, :]

    dom_rows = []
    occ_rows = []
    for offset in range(PARTNERS):
        start = ((occ_pos + offset) % occ_count * aux_count + aux_pos) * OCC_DEV
        dom_rows.append(lax.dynamic_slice_in_dim(domains, start, OCC_DEV, 0))
        occ_rows.append(lax.dynamic_slice_in_dim(occ_energy, start, OCC_DEV, 0))
    vir_rows, vir_cols = energies(jnp.concatenate(dom_rows, axis=0), vir_energy)
    partner_occ = jnp.concatenate(occ_rows, axis=0)

    twin, direct, far, last, late = routes(occ_count)
    is_late = functools.reduce(jnp.logical_or, [occ_pos == n for n in late], jnp.bool_(False))
    is_late = is_late.astype(jnp.int32).reshape(1)
    owns, nears, sets, swaps, thirds = [], [], [], [], []
    transform = functools.partial(transformed, rows_of, own_domains, vir_coef, pos, aux_count)
    sent = [None] * aux_count
    for step in list(range(1, aux_count)) + [0]:
        sent[step] = transform(0, step, 1, [])[0]
    after = [sent[0], vir_rows, partner_occ]
    pieces = [sent[0]] + [along_aux(sent[step], step) for step in range(1, aux_count)]
    for chunk in range(OCC_DEV):
        coming = []
        if chunk + 1 < OCC_DEV:
            sent = transform(chunk + 1, 0, aux_count, after)
            coming = [sent[0]] + [along_aux(sent[step], step) for step in range(1, aux_count)]
        own = stacked(pieces, nears[-1:] + thirds[-1:] + swaps[-2:-1] + coming[:1])
        near = lax.ppermute(own, "occ", direct)
        third = lax.ppermute(own, "occ", far)
        late_near = lax.ppermute(third, "occ", last) if last else near
        both = with_next(own, near, late_near, is_late, coming[1:])
        swap = lax.ppermute(both, "occ", twin)
        for kind, value in zip((owns, nears, sets, swaps, thirds), (own, near, both, swap, third)):
            kind.append(value)
        pieces, after = coming, [own]
    blocks = sets + swaps + thirds
    live = pair_count[0]
    codes = pair_code[0, 0]
    results = []
    for chunk in range(OCC_DEV):
        pieces = densities(
            chunk, aux_count, live, codes, odd, partner_occ, owns[chunk], vir_cols, vir_rows, blocks
        )
        results += [pieces[0]] + [along_aux(pieces[step], -step) for step in range(1, aux_count)]
    return assembled(results, pos, aux_count)


def routes(count):
    chips = count // 2
    twin = [(n, n ^ 1) for n in range(count)]
    turned = [c for c in range(0, chips, 2)] if chips == 4 else []
    direct = [(n, (n - 2) % count) for n in range(count) if not (n % 2 and n // 2 in turned)]
    far = [((n + 3) % count, n) for n in range(1, count, 2)]
    far += [(2 * c + 1, 2 * ((c + 2) % chips)) for c in turned]
    last = [(2 * ((c + 2) % chips), 2 * ((c - 1) % chips) + 1) for c in turned]
    late = [target for _, target in last]
    return twin, direct, far, last, late


def solution(mesh):
    placed = (
        P("aux", "occ", None),
        P("aux", "occ"),
        P(),
        P(),
        P(),
        P(),
        P("occ", "aux"),
        P("occ", "aux", None),
    )
    return jax.shard_map(
        body, mesh=mesh, in_specs=placed, out_specs=P("aux", "occ", None), check_vma=False
    )
```

```python
import functools

import jax
import jax.numpy as jnp
from jax import lax
from jax.experimental import pallas as pl
from jax.experimental.pallas import tpu as pltpu
from jax.sharding import PartitionSpec as P

BLK = 64
OCC_DEV = 4
PARTNERS = 4
ROWS = 16
MIB = 1024 * 1024


def sort_kernel(mask_ref, aux_ref, occ_ref, x_ref, dom_ref, out_ref, own_ref, place_ref):
    step = pl.program_id(0)
    block, orbitals, basis = x_ref.shape
    width = orbitals * ROWS
    place_ref[0] = aux_ref[0]
    place_ref[1] = occ_ref[0]
    start = pl.multiple_of(occ_ref[0] * orbitals, 8)
    own_ref[:, 0, :] = dom_ref[pl.ds(start, orbitals), :]
    row = lax.broadcasted_iota(jnp.int32, (ROWS, width), 0)
    col = lax.broadcasted_iota(jnp.int32, (ROWS, width), 1)
    spread = jnp.concatenate(
        [
            jnp.where(
                col == row * orbitals + orbital, mask_ref[step * block // BLK, orbital].astype(jnp.float32), 0.0
            )
            for orbital in range(orbitals)
        ],
        axis=0,
    ).astype(jnp.bfloat16)
    for part in range(block // ROWS):
        span = slice(part * ROWS, (part + 1) * ROWS)
        moved = jnp.dot(spread, x_ref[span].reshape(width, basis), preferred_element_type=jnp.float32)
        out_ref[:, span, :] = moved.astype(jnp.bfloat16).reshape(orbitals, ROWS, basis)


def sorted_rows(half_ints, block_mask, domains, aux_pos, occ_pos):
    rows, orbitals, basis = half_ints.shape
    virs = domains.shape[1]
    block = BLK // 2
    smem = pl.BlockSpec(memory_space=pltpu.SMEM)
    return pl.pallas_call(
        sort_kernel,
        grid=(rows // block,),
        in_specs=[
            smem,
            smem,
            smem,
            pl.BlockSpec((block, orbitals, basis), lambda g: (g, 0, 0)),
            pl.BlockSpec(domains.shape, lambda g: (0, 0)),
        ],
        out_specs=[
            pl.BlockSpec((orbitals, block, basis), lambda g: (0, g, 0)),
            pl.BlockSpec((orbitals, 1, virs), lambda g: (0, 0, 0)),
            smem,
        ],
        out_shape=[
            jax.ShapeDtypeStruct((orbitals, rows, basis), jnp.bfloat16),
            jax.ShapeDtypeStruct((orbitals, 1, virs), jnp.int32),
            jax.ShapeDtypeStruct((2,), jnp.int32),
        ],
        compiler_params=pltpu.CompilerParams(vmem_limit_bytes=40 * MIB),
        cost_estimate=pl.CostEstimate(
            flops=2 * rows * orbitals * basis * orbitals * ROWS,
            bytes_accessed=4 * rows * orbitals * basis,
            transcendentals=0,
        ),
        name="sort_rows",
    )(block_mask, aux_pos, occ_pos, half_ints, domains)


def transform_kernel(count, after, pos_ref, x_ref, dom_ref, coef_ref, *refs):
    out_refs = refs[after:]
    step = pl.program_id(0)
    tile = 512
    whole = coef_ref.shape[1]
    dom = dom_ref[...]
    total = None
    for part in range(whole // tile):
        full = jnp.dot(
            x_ref[...], coef_ref[:, part * tile : (part + 1) * tile], preferred_element_type=jnp.float32
        ).astype(jnp.bfloat16)
        row = lax.broadcasted_iota(jnp.int32, (tile, dom.shape[1]), 0) + part * tile
        pick = jnp.where(row == dom, 1.0, 0.0).astype(jnp.bfloat16)
        term = jnp.dot(full, pick, preferred_element_type=jnp.float32)
        total = term if total is None else total + term
    total = total.astype(jnp.bfloat16)
    for index in range(count):
        @pl.when(step == index)
        def _():
            out_refs[index][...] = total


def transformed(rows_of, own_domains, vir_coef, aux_pos, aux_count, chunk, first, count, after):
    orbitals, rows, basis = rows_of.shape
    virs = own_domains.shape[2]
    whole = vir_coef.shape[1]

    def orbital(step, pos_ref):
        return lax.rem(pos_ref[0] + first + step, aux_count) * OCC_DEV + chunk

    return pl.pallas_call(
        functools.partial(transform_kernel, count, len(after)),
        grid_spec=pltpu.PrefetchScalarGridSpec(
            num_scalar_prefetch=1,
            grid=(count,),
            in_specs=[
                pl.BlockSpec((None, rows, basis), lambda g, pos: (orbital(g, pos), 0, 0)),
                pl.BlockSpec((None, 1, virs), lambda g, pos: (orbital(g, pos), 0, 0)),
                pl.BlockSpec((basis, whole), lambda g, pos: (0, 0), pipeline_mode=pl.Buffered(1)),
            ]
            + [pl.BlockSpec(memory_space=pl.ANY)] * len(after),
            out_specs=[pl.BlockSpec((rows, virs), lambda g, pos: (0, 0)) for _ in range(count)],
        ),
        out_shape=[jax.ShapeDtypeStruct((rows, virs), jnp.bfloat16) for _ in range(count)],
        compiler_params=pltpu.CompilerParams(vmem_limit_bytes=20 * MIB),
        cost_estimate=pl.CostEstimate(
            flops=2 * count * rows * whole * (basis + virs),
            bytes_accessed=2 * (count * rows * (basis + virs) + basis * whole),
            transcendentals=0,
        ),
        name="transform",
    )(aux_pos, rows_of, own_domains, vir_coef, *after)


def join_kernel(count, *refs):
    out = refs[-1]
    rows = refs[0].shape[0]
    for index in range(count):
        out[index * rows : (index + 1) * rows, :] = refs[index][...]


def stacked(pieces, after):
    rows, virs = pieces[0].shape
    count = len(pieces)
    return pl.pallas_call(
        functools.partial(join_kernel, count),
        in_specs=[pl.BlockSpec((rows, virs), lambda: (0, 0))] * count
        + [pl.BlockSpec(memory_space=pl.ANY)] * len(after),
        out_specs=pl.BlockSpec((count * rows, virs), lambda: (0, 0)),
        out_shape=jax.ShapeDtypeStruct((count * rows, virs), pieces[0].dtype),
        compiler_params=pltpu.CompilerParams(vmem_limit_bytes=16 * MIB),
        cost_estimate=pl.CostEstimate(flops=0, bytes_accessed=4 * count * rows * virs, transcendentals=0),
        name="join",
    )(*pieces, *after)


def pick_kernel(late, place_ref, own_ref, near_ref, late_ref, *refs):
    out = refs[-1]
    is_late = functools.reduce(jnp.logical_or, [place_ref[1] == n for n in late], place_ref[1] < 0)
    out[0] = own_ref[...]

    @pl.when(jnp.logical_not(is_late))
    def _():
        out[1] = near_ref[...]

    @pl.when(is_late)
    def _():
        out[1] = late_ref[...]


def with_next(own, near, late_near, late, place, after):
    rows, virs = own.shape
    block = rows // 4
    return pl.pallas_call(
        functools.partial(pick_kernel, late),
        grid=(rows // block,),
        in_specs=[pl.BlockSpec(memory_space=pltpu.SMEM)]
        + [pl.BlockSpec((block, virs), lambda g: (g, 0))] * 3
        + [pl.BlockSpec(memory_space=pl.ANY)] * len(after),
        out_specs=pl.BlockSpec((2, block, virs), lambda g: (0, g, 0)),
        out_shape=jax.ShapeDtypeStruct((2, rows, virs), own.dtype),
        compiler_params=pltpu.CompilerParams(vmem_limit_bytes=16 * MIB),
        cost_estimate=pl.CostEstimate(flops=0, bytes_accessed=10 * rows * virs, transcendentals=0),
        name="pick",
    )(place, own, near, late_near, *after)


def slot_orbital(place_ref, aux_count, occ_count, slot):
    block = lax.rem(place_ref[1] + slot // OCC_DEV, occ_count) * aux_count + place_ref[0]
    return block * OCC_DEV + slot % OCC_DEV


def energy_kernel(aux_count, occ_count, place_ref, dom_ref, table_ref, row_ref, col_ref):
    slots, _, virs = row_ref.shape
    lanes = table_ref.shape[1]
    rows = []
    for slot in range(slots):
        orbital = slot_orbital(place_ref, aux_count, occ_count, slot)
        rows.append(dom_ref[pl.ds(orbital, 1), :])
    doms = jnp.concatenate(rows, axis=0)
    for part in range(virs // lanes):
        span = slice(part * lanes, (part + 1) * lanes)
        dom = doms[:, span]
        high, low = dom // lanes, dom % lanes
        total = jnp.zeros((slots, lanes), jnp.float32)
        for line in range(table_ref.shape[0]):
            table = jnp.broadcast_to(table_ref[line : line + 1, :], (slots, lanes))
            found = jnp.take_along_axis(table, low, axis=1, mode="promise_in_bounds")
            total = jnp.where(high == line, found, total)
        row_ref[:, 0, span] = total
        col_ref[span, :] = total.T


def energies(place, domains, vir_energy, aux_count, occ_count):
    slots, virs = PARTNERS * OCC_DEV, domains.shape[1]
    vmem = pl.BlockSpec(memory_space=pltpu.VMEM)
    return pl.pallas_call(
        functools.partial(energy_kernel, aux_count, occ_count),
        in_specs=[pl.BlockSpec(memory_space=pltpu.SMEM), vmem, vmem],
        out_specs=[vmem, vmem],
        out_shape=[
            jax.ShapeDtypeStruct((slots, 1, virs), jnp.float32),
            jax.ShapeDtypeStruct((virs, slots), jnp.float32),
        ],
        compiler_params=pltpu.CompilerParams(vmem_limit_bytes=8 * MIB),
        cost_estimate=pl.CostEstimate(flops=0, bytes_accessed=4 * domains.size, transcendentals=0),
        name="energies",
    )(place, domains, vir_energy.reshape(-1, 128))


def pair_kernel(chunk, count, occ_count, live_ref, code_ref, place_ref, occ_ref, own_ref, col_ref, row_ref, *refs):
    sets = 3
    blocks = refs[: sets * OCC_DEV]
    outs = refs[sets * OCC_DEV : sets * OCC_DEV + count]
    turned, total, held, sems, todo = refs[sets * OCC_DEV + count :]
    span = PARTNERS * OCC_DEV
    slots = code_ref.shape[0]
    odd = place_ref[1] % 2

    def scan(slot, found):
        code = code_ref[slot]
        mine = (slot < live_ref[0, 0]) & (code // span == chunk)

        @pl.when(mine)
        def _():
            todo[found] = code % span

        return found + mine.astype(jnp.int32)

    pairs = lax.fori_loop(0, slots, scan, jnp.int32(0))

    def source(slot):
        offset = slot // OCC_DEV
        one = jnp.where(odd == 1, 3, 2)
        three = jnp.where(odd == 1, 4, 3)
        kind = jnp.where(offset == 0, 0, jnp.where(offset == 1, one, jnp.where(offset == 2, 1, three)))
        return kind * OCC_DEV + slot % OCC_DEV

    def fetch(index):
        place = source(todo[index])
        buffer = lax.rem(index, 2)
        for kind in range(5):
            for orbital in range(OCC_DEV):
                block = blocks[kind // 2 * OCC_DEV + orbital]
                block = block.at[kind % 2] if kind < 4 else block

                @pl.when(place == kind * OCC_DEV + orbital)
                def _():
                    pltpu.make_async_copy(block, held.at[buffer], sems.at[buffer]).start()

    @pl.when(pairs > 0)
    def _():
        fetch(0)
        turned[...] = own_ref[...].T

    total[...] = jnp.zeros_like(total)

    def step(index, carry):
        @pl.when(index + 1 < pairs)
        def _():
            fetch(index + 1)

        buffer = lax.rem(index, 2)
        pltpu.make_async_copy(blocks[0].at[0], held.at[buffer], sems.at[buffer]).wait()
        slot = todo[index]
        energy = lambda which: occ_ref[slot_orbital(place_ref, count, occ_count, which)]
        shift = energy(chunk) + energy(slot)
        other = held[buffer]
        exchange = jnp.dot(turned[...], other, preferred_element_type=jnp.float32)
        denom = (col_ref[:, chunk : chunk + 1] + row_ref[slot]) - shift
        amplitude = (exchange / denom).astype(jnp.bfloat16)
        total[...] += lax.dot_general(
            other, amplitude, (((1,), (1,)), ((), ())), preferred_element_type=jnp.float32
        )
        return carry

    lax.fori_loop(0, pairs, step, jnp.int32(0))
    part = outs[0].shape[0]
    for index, out in enumerate(outs):
        out[...] = total[index * part : (index + 1) * part, :].astype(jnp.bfloat16)


def densities(chunk, count, occ_count, live, codes, place, occ_energy, own, own_vir, vir_rows, blocks):
    aux, virs = own.shape
    rows = aux // count
    whole = lambda shape: pl.BlockSpec(shape, lambda: (0,) * len(shape))
    smem = pl.BlockSpec(memory_space=pltpu.SMEM)
    return pl.pallas_call(
        functools.partial(pair_kernel, chunk, count, occ_count),
        in_specs=[smem, smem, smem, smem, whole(own.shape), whole(own_vir.shape), whole(vir_rows.shape)]
        + [pl.BlockSpec(memory_space=pl.ANY)] * len(blocks),
        out_specs=[whole((rows, virs))] * count,
        out_shape=[jax.ShapeDtypeStruct((rows, virs), jnp.bfloat16)] * count,
        scratch_shapes=[
            pltpu.VMEM((virs, aux), jnp.bfloat16),
            pltpu.VMEM((aux, virs), jnp.float32),
            pltpu.VMEM((2, aux, virs), jnp.bfloat16),
            pltpu.SemaphoreType.DMA((2,)),
            pltpu.SMEM((codes.shape[0],), jnp.int32),
        ],
        compiler_params=pltpu.CompilerParams(vmem_limit_bytes=20 * MIB),
        cost_estimate=pl.CostEstimate(
            flops=4 * 4 * aux * virs * virs, bytes_accessed=6 * aux * virs, transcendentals=0
        ),
        name="pairs",
    )(live, codes, place, occ_energy, own, own_vir, vir_rows, *blocks)


def spread_kernel(count, pos_ref, *refs):
    pieces, out = refs[:-1], refs[-1]
    orbitals = count * OCC_DEV
    width = orbitals * ROWS
    row = lax.broadcasted_iota(jnp.int32, (width, width), 0)
    col = lax.broadcasted_iota(jnp.int32, (width, width), 1)
    group = col // ROWS
    place = lax.rem(pos_ref[0] + group % count, count) * OCC_DEV + group // count
    hit = jnp.where((row % orbitals == place) & (row // orbitals == col % ROWS), 1.0, 0.0).astype(jnp.bfloat16)
    for part in range(out.shape[0] // ROWS):
        span = pl.ds(part * ROWS, ROWS)
        rows = jnp.concatenate([piece[span, :] for piece in pieces], axis=0)
        moved = jnp.dot(hit, rows, preferred_element_type=jnp.float32).astype(jnp.bfloat16)
        out[span] = moved.reshape(ROWS, orbitals, -1)


def assembled(pieces, aux_pos, count):
    rows, virs = pieces[0].shape
    orbitals = count * OCC_DEV
    block = 4 * ROWS
    return pl.pallas_call(
        functools.partial(spread_kernel, count),
        grid_spec=pltpu.PrefetchScalarGridSpec(
            num_scalar_prefetch=1,
            grid=(rows // block,),
            in_specs=[pl.BlockSpec((block, virs), lambda g, pos: (g, 0))] * len(pieces),
            out_specs=pl.BlockSpec((block, orbitals, virs), lambda g, pos: (g, 0, 0)),
        ),
        out_shape=jax.ShapeDtypeStruct((rows, orbitals, virs), jnp.bfloat16),
        compiler_params=pltpu.CompilerParams(vmem_limit_bytes=20 * MIB),
        cost_estimate=pl.CostEstimate(
            flops=2 * rows * orbitals * virs * orbitals * ROWS,
            bytes_accessed=4 * rows * orbitals * virs,
            transcendentals=0,
        ),
        name="assemble",
    )(aux_pos, *pieces)


def body(half_ints, block_mask, vir_coef, domains, vir_energy, occ_energy, pair_count, pair_code):
    aux_count = lax.axis_size("aux")
    occ_count = lax.axis_size("occ")
    aux_pos = lax.axis_index("aux")
    occ_pos = lax.axis_index("occ")

    def along_aux(value, steps):
        return lax.ppermute(value, "aux", [(z, (z + steps) % aux_count) for z in range(aux_count)])

    rows_of, own_domains, place = sorted_rows(
        half_ints, block_mask, domains, aux_pos.astype(jnp.int32).reshape(1), occ_pos.astype(jnp.int32).reshape(1)
    )
    vir_rows, vir_cols = energies(place, domains, vir_energy, aux_count, occ_count)
    twin, direct, far, last, late = routes(occ_count)
    owns, nears, thirds, lates, sets, swaps = [], [], [], [], [], []
    transform = functools.partial(transformed, rows_of, own_domains, vir_coef, place, aux_count)
    sent = [None] * aux_count
    for step in list(range(1, aux_count)) + [0]:
        sent[step] = transform(0, step, 1, [])[0]
    after = [sent[0]]
    pieces = [sent[0]] + [along_aux(sent[step], step) for step in range(1, aux_count)]
    for chunk in range(OCC_DEV + 1):
        coming = []
        if chunk + 1 < OCC_DEV:
            sent = transform(chunk + 1, 0, aux_count, after)
            coming = [sent[0]] + [along_aux(sent[step], step) for step in range(1, aux_count)]
        if chunk < OCC_DEV:
            own = stacked(pieces, nears[-1:] + thirds[-1:] + lates[-2:-1] + coming[:1])
            near = lax.ppermute(own, "occ", direct)
            third = lax.ppermute(own, "occ", far)
            owns.append(own)
            nears.append(near)
            thirds.append(third)
            lates.append(lax.ppermute(third, "occ", last) if last else near)
        if chunk >= 1:
            waits = coming[1:] + nears[-1:] if coming else []
            both = with_next(owns[chunk - 1], nears[chunk - 1], lates[chunk - 1], late, place, waits)
            sets.append(both)
            swaps.append(lax.ppermute(both, "occ", twin))
        pieces, after = coming, [own, vir_rows]
    blocks = sets + swaps + thirds
    codes = pair_code[0, 0]
    results = []
    for chunk in range(OCC_DEV):
        pieces = densities(
            chunk, aux_count, occ_count, pair_count, codes, place, occ_energy, owns[chunk], vir_cols, vir_rows, blocks
        )
        results += [pieces[0]] + [along_aux(pieces[step], -step) for step in range(1, aux_count)]
    return assembled(results, place, aux_count)


def routes(count):
    chips = count // 2
    twin = [(n, n ^ 1) for n in range(count)]
    turned = [c for c in range(0, chips, 2)] if chips == 4 else []
    direct = [(n, (n - 2) % count) for n in range(count) if n % 2 or n // 2 not in turned]
    far = [((n + 3) % count, n) for n in range(1, count, 2)]
    last = [(2 * ((c + 2) % chips) + 1, 2 * ((c - 1) % chips)) for c in turned]
    late = [target for _, target in last]
    return twin, direct, far, last, late


def solution(mesh):
    placed = (
        P("aux", "occ", None),
        P("aux", "occ"),
        P(),
        P(),
        P(),
        P(),
        P("occ", "aux"),
        P("occ", "aux", None),
    )
    return jax.shard_map(
        body, mesh=mesh, in_specs=placed, out_specs=P("aux", "occ", None), check_vma=False
    )
```

```python
import functools

import jax
import jax.numpy as jnp
from jax import lax
from jax.experimental import pallas as pl
from jax.experimental.pallas import tpu as pltpu
from jax.sharding import PartitionSpec as P

BLK = 64
OCC_DEV = 4
PARTNERS = 4
ROWS = 16
MIB = 1024 * 1024


def sort_kernel(mask_ref, aux_ref, occ_ref, x_ref, out_ref, place_ref):
    step = pl.program_id(0)
    block, orbitals, basis = x_ref.shape
    width = orbitals * ROWS
    place_ref[0] = aux_ref[0]
    place_ref[1] = occ_ref[0]
    row = lax.broadcasted_iota(jnp.int32, (ROWS, width), 0)
    col = lax.broadcasted_iota(jnp.int32, (ROWS, width), 1)
    spread = jnp.concatenate(
        [
            jnp.where(
                col == row * orbitals + orbital, mask_ref[step * block // BLK, orbital].astype(jnp.float32), 0.0
            )
            for orbital in range(orbitals)
        ],
        axis=0,
    ).astype(jnp.bfloat16)
    for part in range(block // ROWS):
        span = slice(part * ROWS, (part + 1) * ROWS)
        moved = jnp.dot(spread, x_ref[span].reshape(width, basis), preferred_element_type=jnp.float32)
        out_ref[:, span, :] = moved.astype(jnp.bfloat16).reshape(orbitals, ROWS, basis)


def sorted_rows(half_ints, block_mask, aux_pos, occ_pos):
    rows, orbitals, basis = half_ints.shape
    block = BLK
    smem = pl.BlockSpec(memory_space=pltpu.SMEM)
    return pl.pallas_call(
        sort_kernel,
        grid=(rows // block,),
        in_specs=[
            smem,
            smem,
            smem,
            pl.BlockSpec((block, orbitals, basis), lambda g: (g, 0, 0)),
        ],
        out_specs=[
            pl.BlockSpec((orbitals, block, basis), lambda g: (0, g, 0)),
            smem,
        ],
        out_shape=[
            jax.ShapeDtypeStruct((orbitals, rows, basis), jnp.bfloat16),
            jax.ShapeDtypeStruct((2,), jnp.int32),
        ],
        compiler_params=pltpu.CompilerParams(vmem_limit_bytes=40 * MIB),
        cost_estimate=pl.CostEstimate(
            flops=2 * rows * orbitals * basis * orbitals * ROWS,
            bytes_accessed=4 * rows * orbitals * basis,
            transcendentals=0,
        ),
        name="sort_rows",
    )(block_mask, aux_pos, occ_pos, half_ints)


def transform_kernel(count, orbitals, orbital, after, pos_ref, x_ref, dom_ref, coef_ref, *refs):
    out_refs = refs[after:]
    step = pl.program_id(0)
    tile = 512
    whole = coef_ref.shape[1]
    dom = dom_ref[pl.ds(pos_ref[1] * orbitals + orbital(step, pos_ref), 1), :]
    total = None
    for part in range(whole // tile):
        full = jnp.dot(
            x_ref[...], coef_ref[:, part * tile : (part + 1) * tile], preferred_element_type=jnp.float32
        ).astype(jnp.bfloat16)
        row = lax.broadcasted_iota(jnp.int32, (tile, dom.shape[1]), 0) + part * tile
        pick = jnp.where(row == dom, 1.0, 0.0).astype(jnp.bfloat16)
        term = jnp.dot(full, pick, preferred_element_type=jnp.float32)
        total = term if total is None else total + term
    total = total.astype(jnp.bfloat16)
    for index in range(count):
        @pl.when(step == index)
        def _():
            out_refs[index][...] = total


def transformed(rows_of, domains, vir_coef, place, aux_count, chunk, chunk_step, first, first_step, count, after):
    orbitals, rows, basis = rows_of.shape
    virs = domains.shape[1]
    whole = vir_coef.shape[1]

    def orbital(step, pos_ref):
        return lax.rem(pos_ref[0] + first + step * first_step, aux_count) * OCC_DEV + chunk + step * chunk_step

    return pl.pallas_call(
        functools.partial(transform_kernel, count, orbitals, orbital, len(after)),
        grid_spec=pltpu.PrefetchScalarGridSpec(
            num_scalar_prefetch=1,
            grid=(count,),
            in_specs=[
                pl.BlockSpec((None, rows, basis), lambda g, pos: (orbital(g, pos), 0, 0)),
                pl.BlockSpec(domains.shape, lambda g, pos: (0, 0)),
                pl.BlockSpec((basis, whole), lambda g, pos: (0, 0), pipeline_mode=pl.Buffered(1)),
            ]
            + [pl.BlockSpec(memory_space=pl.ANY)] * len(after),
            out_specs=[pl.BlockSpec((rows, virs), lambda g, pos: (0, 0)) for _ in range(count)],
        ),
        out_shape=[jax.ShapeDtypeStruct((rows, virs), jnp.bfloat16) for _ in range(count)],
        compiler_params=pltpu.CompilerParams(vmem_limit_bytes=20 * MIB),
        cost_estimate=pl.CostEstimate(
            flops=2 * count * rows * whole * (basis + virs),
            bytes_accessed=2 * (count * rows * (basis + virs) + basis * whole),
            transcendentals=0,
        ),
        name="transform",
    )(place, rows_of, domains, vir_coef, *after)


def join_kernel(count, place_ref, *refs):
    out = refs[count]
    rows = refs[0].shape[0]
    for index in range(count):
        out[index * rows : (index + 1) * rows, :] = refs[index][...]


def join_pass_kernel(count, place_ref, *refs):
    out, onward = refs[-2:]
    rows = refs[0].shape[0]
    for index in range(count):
        out[index * rows : (index + 1) * rows, :] = refs[index][...]

    @pl.when(place_ref[1] % 2 == 0)
    def _():
        onward[...] = out[...]

    @pl.when(place_ref[1] % 2 == 1)
    def _():
        onward[...] = refs[count][...]


def stacked(pieces, place, held, after):
    rows, virs = pieces[0].shape
    count = len(pieces)
    whole = pl.BlockSpec((count * rows, virs), lambda: (0, 0))
    shape = jax.ShapeDtypeStruct((count * rows, virs), pieces[0].dtype)
    kernel = join_pass_kernel if held else join_kernel
    outs = 1 + len(held)

    def entry(place_ref, *refs):
        kernel(count, place_ref, *refs[: count + len(held)], *refs[-outs:])

    return pl.pallas_call(
        entry,
        in_specs=[pl.BlockSpec(memory_space=pltpu.SMEM)]
        + [pl.BlockSpec((rows, virs), lambda: (0, 0))] * count
        + [whole] * len(held)
        + [pl.BlockSpec(memory_space=pl.ANY)] * len(after),
        out_specs=[whole] * outs,
        out_shape=[shape] * outs,
        compiler_params=pltpu.CompilerParams(vmem_limit_bytes=20 * MIB),
        cost_estimate=pl.CostEstimate(flops=0, bytes_accessed=4 * count * rows * virs * outs, transcendentals=0),
        name="join",
    )(place, *pieces, *held, *after)


def pick_kernel(late, place_ref, own_ref, near_ref, late_ref, *refs):
    out = refs[-1]
    is_late = functools.reduce(jnp.logical_or, [place_ref[1] == n for n in late], place_ref[1] < 0)
    out[0] = own_ref[...]

    @pl.when(jnp.logical_not(is_late))
    def _():
        out[1] = near_ref[...]

    @pl.when(is_late)
    def _():
        out[1] = late_ref[...]


def with_next(own, near, late_near, late, place, after):
    rows, virs = own.shape
    block = rows // 2
    return pl.pallas_call(
        functools.partial(pick_kernel, late),
        grid=(rows // block,),
        in_specs=[pl.BlockSpec(memory_space=pltpu.SMEM)]
        + [pl.BlockSpec((block, virs), lambda g: (g, 0))] * 3
        + [pl.BlockSpec(memory_space=pl.ANY)] * len(after),
        out_specs=pl.BlockSpec((2, block, virs), lambda g: (0, g, 0)),
        out_shape=jax.ShapeDtypeStruct((2, rows, virs), own.dtype),
        compiler_params=pltpu.CompilerParams(vmem_limit_bytes=16 * MIB),
        cost_estimate=pl.CostEstimate(flops=0, bytes_accessed=10 * rows * virs, transcendentals=0),
        name="pick",
    )(place, own, near, late_near, *after)


def slot_orbital(place_ref, aux_count, occ_count, slot):
    block = lax.rem(place_ref[1] + slot // OCC_DEV, occ_count) * aux_count + place_ref[0]
    return block * OCC_DEV + slot % OCC_DEV


def energy_kernel(aux_count, occ_count, place_ref, dom_ref, table_ref, row_ref, col_ref):
    slots, _, virs = row_ref.shape
    lanes = table_ref.shape[1]
    rows = []
    for slot in range(slots):
        orbital = slot_orbital(place_ref, aux_count, occ_count, slot)
        rows.append(dom_ref[pl.ds(orbital, 1), :])
    doms = jnp.concatenate(rows, axis=0)
    for part in range(virs // lanes):
        span = slice(part * lanes, (part + 1) * lanes)
        dom = doms[:, span]
        high, low = dom // lanes, dom % lanes
        total = jnp.zeros((slots, lanes), jnp.float32)
        for line in range(table_ref.shape[0]):
            table = jnp.broadcast_to(table_ref[line : line + 1, :], (slots, lanes))
            found = jnp.take_along_axis(table, low, axis=1, mode="promise_in_bounds")
            total = jnp.where(high == line, found, total)
        row_ref[:, 0, span] = total
        col_ref[span, :] = total.T


def energies(place, domains, vir_energy, aux_count, occ_count):
    slots, virs = PARTNERS * OCC_DEV, domains.shape[1]
    vmem = pl.BlockSpec(memory_space=pltpu.VMEM)
    return pl.pallas_call(
        functools.partial(energy_kernel, aux_count, occ_count),
        in_specs=[pl.BlockSpec(memory_space=pltpu.SMEM), vmem, vmem],
        out_specs=[vmem, vmem],
        out_shape=[
            jax.ShapeDtypeStruct((slots, 1, virs), jnp.float32),
            jax.ShapeDtypeStruct((virs, slots), jnp.float32),
        ],
        compiler_params=pltpu.CompilerParams(vmem_limit_bytes=8 * MIB),
        cost_estimate=pl.CostEstimate(flops=0, bytes_accessed=4 * domains.size, transcendentals=0),
        name="energies",
    )(place, domains, vir_energy.reshape(-1, 128))


def pair_kernel(chunk, count, occ_count, live_ref, code_ref, place_ref, occ_ref, *refs):
    own_refs, (col_ref, row_ref), refs = refs[:count], refs[count : count + 2], refs[count + 2 :]
    sets = 3
    blocks = refs[: sets * OCC_DEV]
    outs = refs[sets * OCC_DEV : sets * OCC_DEV + count]
    turned, total, held, sems, todo = refs[sets * OCC_DEV + count :]
    split = own_refs[0].shape[0]
    aux = split * count
    span = PARTNERS * OCC_DEV
    slots = code_ref.shape[0]
    odd = place_ref[1] % 2

    def scan(slot, found):
        code = code_ref[slot]
        mine = (slot < live_ref[0, 0]) & (code // span == chunk)

        @pl.when(mine)
        def _():
            todo[found] = code % span

        return found + mine.astype(jnp.int32)

    pairs = lax.fori_loop(0, slots, scan, jnp.int32(0))

    def source(slot):
        offset = slot // OCC_DEV
        one = jnp.where(odd == 1, 3, 2)
        three = jnp.where(odd == 1, 4, 3)
        kind = jnp.where(offset == 0, 0, jnp.where(offset == 1, one, jnp.where(offset == 2, 1, three)))
        return kind * OCC_DEV + slot % OCC_DEV

    def fetch(index):
        place = source(todo[index])
        buffer = lax.rem(index, 2)
        for kind in range(5):
            parts = [blocks[kind // 2 * OCC_DEV + orbital] for orbital in range(OCC_DEV)]
            parts = [part.at[kind % 2] for part in parts] if kind < 4 else parts
            for orbital in range(OCC_DEV):
                @pl.when(place == kind * OCC_DEV + orbital)
                def _():
                    if orbital == 0:
                        first, rest = parts[0].at[pl.ds(0, split)], parts[0].at[pl.ds(split, aux - split)]
                    else:
                        start = aux if orbital == 1 else aux - split
                        first = parts[orbital - 1].at[pl.ds(start, split)]
                        rest = parts[orbital].at[pl.ds(0, aux - split)]
                    pltpu.make_async_copy(first, held.at[buffer, pl.ds(0, split)], sems.at[buffer, 0]).start()
                    pltpu.make_async_copy(rest, held.at[buffer, pl.ds(split, aux - split)], sems.at[buffer, 1]).start()

    @pl.when(pairs > 0)
    def _():
        fetch(0)
        for index, own_ref in enumerate(own_refs):
            turned[:, index * split : (index + 1) * split] = own_ref[...].T

    total[...] = jnp.zeros_like(total)

    def step(index, carry):
        @pl.when(index + 1 < pairs)
        def _():
            fetch(index + 1)

        buffer = lax.rem(index, 2)
        first, rest = held.at[buffer, pl.ds(0, split)], held.at[buffer, pl.ds(split, aux - split)]
        pltpu.make_async_copy(blocks[0].at[0, pl.ds(0, split)], first, sems.at[buffer, 0]).wait()
        pltpu.make_async_copy(blocks[0].at[0, pl.ds(split, aux - split)], rest, sems.at[buffer, 1]).wait()
        slot = todo[index]
        energy = lambda which: occ_ref[slot_orbital(place_ref, count, occ_count, which)]
        shift = energy(chunk) + energy(slot)
        other = held[buffer]
        exchange = jnp.dot(turned[...], other, preferred_element_type=jnp.float32)
        denom = (col_ref[:, chunk : chunk + 1] + row_ref[slot]) - shift
        amplitude = (exchange / denom).astype(jnp.bfloat16)
        total[...] += lax.dot_general(
            other, amplitude, (((1,), (1,)), ((), ())), preferred_element_type=jnp.float32
        )
        return carry

    lax.fori_loop(0, pairs, step, jnp.int32(0))
    part = outs[0].shape[0]
    for index, out in enumerate(outs):
        out[...] = total[index * part : (index + 1) * part, :].astype(jnp.bfloat16)


def densities(chunk, count, occ_count, live, codes, place, occ_energy, own, own_vir, vir_rows, blocks):
    rows, virs = own[0].shape
    aux = rows * count
    whole = lambda shape: pl.BlockSpec(shape, lambda: (0,) * len(shape))
    smem = pl.BlockSpec(memory_space=pltpu.SMEM)
    return pl.pallas_call(
        functools.partial(pair_kernel, chunk, count, occ_count),
        in_specs=[smem] * 4 + [whole((rows, virs))] * count + [whole(own_vir.shape), whole(vir_rows.shape)]
        + [pl.BlockSpec(memory_space=pl.ANY)] * len(blocks),
        out_specs=[whole((rows, virs))] * count,
        out_shape=[jax.ShapeDtypeStruct((rows, virs), jnp.bfloat16)] * count,
        scratch_shapes=[
            pltpu.VMEM((virs, aux), jnp.bfloat16),
            pltpu.VMEM((aux, virs), jnp.float32),
            pltpu.VMEM((2, aux, virs), jnp.bfloat16),
            pltpu.SemaphoreType.DMA((2, 2)),
            pltpu.SMEM((codes.shape[0],), jnp.int32),
        ],
        compiler_params=pltpu.CompilerParams(vmem_limit_bytes=20 * MIB),
        cost_estimate=pl.CostEstimate(
            flops=4 * 4 * aux * virs * virs, bytes_accessed=6 * aux * virs, transcendentals=0
        ),
        name="pairs",
    )(live, codes, place, occ_energy, *own, own_vir, vir_rows, *blocks)


def spread_kernel(count, pos_ref, *refs):
    pieces, out = refs[:-1], refs[-1]
    orbitals = count * OCC_DEV
    width = orbitals * ROWS
    row = lax.broadcasted_iota(jnp.int32, (width, width), 0)
    col = lax.broadcasted_iota(jnp.int32, (width, width), 1)
    group = col // ROWS
    place = lax.rem(pos_ref[0] + group % count, count) * OCC_DEV + group // count
    hit = jnp.where((row % orbitals == place) & (row // orbitals == col % ROWS), 1.0, 0.0).astype(jnp.bfloat16)
    for part in range(out.shape[0] // ROWS):
        span = pl.ds(part * ROWS, ROWS)
        rows = jnp.concatenate([piece[span, :] for piece in pieces], axis=0)
        moved = jnp.dot(hit, rows, preferred_element_type=jnp.float32).astype(jnp.bfloat16)
        out[span] = moved.reshape(ROWS, orbitals, -1)


def assembled(pieces, aux_pos, count):
    rows, virs = pieces[0].shape
    orbitals = count * OCC_DEV
    block = 4 * ROWS
    return pl.pallas_call(
        functools.partial(spread_kernel, count),
        grid_spec=pltpu.PrefetchScalarGridSpec(
            num_scalar_prefetch=1,
            grid=(rows // block,),
            in_specs=[pl.BlockSpec((block, virs), lambda g, pos: (g, 0))] * len(pieces),
            out_specs=pl.BlockSpec((block, orbitals, virs), lambda g, pos: (g, 0, 0)),
        ),
        out_shape=jax.ShapeDtypeStruct((rows, orbitals, virs), jnp.bfloat16),
        compiler_params=pltpu.CompilerParams(vmem_limit_bytes=20 * MIB),
        cost_estimate=pl.CostEstimate(
            flops=2 * rows * orbitals * virs * orbitals * ROWS,
            bytes_accessed=4 * rows * orbitals * virs,
            transcendentals=0,
        ),
        name="assemble",
    )(aux_pos, *pieces)


def body(half_ints, block_mask, vir_coef, domains, vir_energy, occ_energy, pair_count, pair_code):
    aux_count = lax.axis_size("aux")
    occ_count = lax.axis_size("occ")
    aux_pos = lax.axis_index("aux")
    occ_pos = lax.axis_index("occ")

    def along_aux(value, steps):
        return lax.ppermute(value, "aux", [(z, (z + steps) % aux_count) for z in range(aux_count)])

    rows_of, place = sorted_rows(
        half_ints, block_mask, aux_pos.astype(jnp.int32).reshape(1), occ_pos.astype(jnp.int32).reshape(1)
    )
    vir_rows, vir_cols = energies(place, domains, vir_energy, aux_count, occ_count)
    twin, direct, far, last, late = routes(occ_count)
    transform = functools.partial(transformed, rows_of, domains, vir_coef, place, aux_count)

    order = list(range(1, aux_count)) + [0]
    sent = [None] * aux_count
    for step in order:
        sent[step] = transform(0, 0, step, 0, 1, [])[0]
    pieces = [sent[0]] + [along_aux(sent[step], step) for step in range(1, aux_count)]
    parts, owns, nears, thirds, lates, sets, swaps = [], [], [], [], [], [], []
    after = [sent[0]]
    for chunk in range(OCC_DEV + 1):
        coming = []
        if chunk + 1 < OCC_DEV:
            sent = transform(chunk + 1, 0, 0, 1, aux_count, after)
            coming = [sent[0]] + [along_aux(sent[step], step) for step in range(1, aux_count)]
        if chunk < OCC_DEV:
            parts.append(pieces)
            message = pieces[0 if chunk == 0 else 1 :] + coming[:1]
            rides = bool(last) and 1 < chunk < OCC_DEV - 1
            ready = nears[-1:] + ([] if rides else thirds[-1:] + lates[-1:])
            own, *onward = stacked(message, place, thirds[-1:] if rides else [], ready)
            near = lax.ppermute(own, "occ", direct)
            third = lax.ppermute(onward[0], "occ", far + last) if rides else lax.ppermute(own, "occ", far)
            owns.append(own)
            nears.append(near)
            thirds.append(third)
            if rides:
                lates.append(third)
            if last and chunk != 1:
                onward = stacked([third], place, [], coming[1:3])[0] if coming else third
                lates.append(lax.ppermute(onward, "occ", last))
            if not last:
                lates.append(near)
        if chunk >= 1:
            waits = coming[1:] + nears[-1:] if coming else []
            both = with_next(owns[chunk - 1], nears[chunk - 1], lates[chunk - 1], late, place, waits)
            sets.append(both)
            swaps.append(lax.ppermute(both, "occ", twin))
        pieces, after = coming, [own, vir_rows]
    blocks = sets + swaps + thirds
    codes = pair_code[0, 0]
    results = []
    for chunk in range(OCC_DEV):
        pieces = densities(
            chunk, aux_count, occ_count, pair_count, codes, place, occ_energy, parts[chunk], vir_cols, vir_rows, blocks
        )
        results += [pieces[0]] + [along_aux(pieces[step], -step) for step in range(1, aux_count)]
    return assembled(results, place, aux_count)


def routes(count):
    chips = count // 2
    twin = [(n, n ^ 1) for n in range(count)]
    turned = [c for c in range(0, chips, 2)] if chips == 4 else []
    direct = [(n, (n - 2) % count) for n in range(count) if n % 2 or n // 2 not in turned]
    far = [((n + 3) % count, n) for n in range(1, count, 2)]
    last = [(2 * ((c + 2) % chips) + 1, 2 * ((c - 1) % chips)) for c in turned]
    late = [target for _, target in last]
    return twin, direct, far, last, late


def solution(mesh):
    placed = (
        P("aux", "occ", None),
        P("aux", "occ"),
        P(),
        P(),
        P(),
        P(),
        P("occ", "aux"),
        P("occ", "aux", None),
    )
    return jax.shard_map(
        body, mesh=mesh, in_specs=placed, out_specs=P("aux", "occ", None), check_vma=False
    )
```

```python
import functools

import jax
import jax.numpy as jnp
from jax import lax
from jax.experimental import pallas as pl
from jax.experimental.pallas import tpu as pltpu
from jax.sharding import PartitionSpec as P

BLK = 64
OCC_DEV = 4
PARTNERS = 4
ROWS = 16
MIB = 1024 * 1024


def sort_kernel(mask_ref, aux_ref, occ_ref, x_ref, out_ref, place_ref):
    step = pl.program_id(0)
    block, orbitals, basis = x_ref.shape
    width = orbitals * ROWS
    place_ref[0] = aux_ref[0]
    place_ref[1] = occ_ref[0]
    row = lax.broadcasted_iota(jnp.int32, (ROWS, width), 0)
    col = lax.broadcasted_iota(jnp.int32, (ROWS, width), 1)
    spread = jnp.concatenate(
        [
            jnp.where(
                col == row * orbitals + orbital, mask_ref[step * block // BLK, orbital].astype(jnp.float32), 0.0
            )
            for orbital in range(orbitals)
        ],
        axis=0,
    ).astype(jnp.bfloat16)
    for part in range(block // ROWS):
        span = slice(part * ROWS, (part + 1) * ROWS)
        moved = jnp.dot(spread, x_ref[span].reshape(width, basis), preferred_element_type=jnp.float32)
        out_ref[:, span, :] = moved.astype(jnp.bfloat16).reshape(orbitals, ROWS, basis)


def sorted_rows(half_ints, block_mask, aux_pos, occ_pos):
    rows, orbitals, basis = half_ints.shape
    block = BLK
    smem = pl.BlockSpec(memory_space=pltpu.SMEM)
    return pl.pallas_call(
        sort_kernel,
        grid=(rows // block,),
        in_specs=[
            smem,
            smem,
            smem,
            pl.BlockSpec((block, orbitals, basis), lambda g: (g, 0, 0)),
        ],
        out_specs=[
            pl.BlockSpec((orbitals, block, basis), lambda g: (0, g, 0)),
            smem,
        ],
        out_shape=[
            jax.ShapeDtypeStruct((orbitals, rows, basis), jnp.bfloat16),
            jax.ShapeDtypeStruct((2,), jnp.int32),
        ],
        compiler_params=pltpu.CompilerParams(vmem_limit_bytes=40 * MIB),
        cost_estimate=pl.CostEstimate(
            flops=2 * rows * orbitals * basis * orbitals * ROWS,
            bytes_accessed=4 * rows * orbitals * basis,
            transcendentals=0,
        ),
        name="sort_rows",
    )(block_mask, aux_pos, occ_pos, half_ints)


def transform_kernel(count, orbitals, orbital, after, pos_ref, x_ref, dom_ref, coef_ref, *refs):
    out_refs = refs[after:]
    step = pl.program_id(0)
    tile = 512
    whole = coef_ref.shape[1]
    dom = dom_ref[pl.ds(pos_ref[1] * orbitals + orbital(step, pos_ref), 1), :]
    total = None
    for part in range(whole // tile):
        full = jnp.dot(
            x_ref[...], coef_ref[:, part * tile : (part + 1) * tile], preferred_element_type=jnp.float32
        ).astype(jnp.bfloat16)
        row = lax.broadcasted_iota(jnp.int32, (tile, dom.shape[1]), 0) + part * tile
        pick = jnp.where(row == dom, 1.0, 0.0).astype(jnp.bfloat16)
        term = jnp.dot(full, pick, preferred_element_type=jnp.float32)
        total = term if total is None else total + term
    total = total.astype(jnp.bfloat16)
    for index in range(count):
        @pl.when(step == index)
        def _():
            out_refs[index][...] = total


def transformed(rows_of, domains, vir_coef, place, aux_count, chunk, chunk_step, first, first_step, count, after):
    orbitals, rows, basis = rows_of.shape
    virs = domains.shape[1]
    whole = vir_coef.shape[1]

    def orbital(step, pos_ref):
        return lax.rem(pos_ref[0] + first + step * first_step, aux_count) * OCC_DEV + chunk + step * chunk_step

    return pl.pallas_call(
        functools.partial(transform_kernel, count, orbitals, orbital, len(after)),
        grid_spec=pltpu.PrefetchScalarGridSpec(
            num_scalar_prefetch=1,
            grid=(count,),
            in_specs=[
                pl.BlockSpec((None, rows, basis), lambda g, pos: (orbital(g, pos), 0, 0)),
                pl.BlockSpec(domains.shape, lambda g, pos: (0, 0)),
                pl.BlockSpec((basis, whole), lambda g, pos: (0, 0), pipeline_mode=pl.Buffered(1)),
            ]
            + [pl.BlockSpec(memory_space=pl.ANY)] * len(after),
            out_specs=[pl.BlockSpec((rows, virs), lambda g, pos: (0, 0)) for _ in range(count)],
        ),
        out_shape=[jax.ShapeDtypeStruct((rows, virs), jnp.bfloat16) for _ in range(count)],
        compiler_params=pltpu.CompilerParams(vmem_limit_bytes=20 * MIB),
        cost_estimate=pl.CostEstimate(
            flops=2 * count * rows * whole * (basis + virs),
            bytes_accessed=2 * (count * rows * (basis + virs) + basis * whole),
            transcendentals=0,
        ),
        name="transform",
    )(place, rows_of, domains, vir_coef, *after)


def join_kernel(count, place_ref, *refs):
    out = refs[count]
    rows = refs[0].shape[0]
    for index in range(count):
        out[index * rows : (index + 1) * rows, :] = refs[index][...]


def join_pass_kernel(count, place_ref, *refs):
    out, onward = refs[-2:]
    rows = refs[0].shape[0]
    for index in range(count):
        out[index * rows : (index + 1) * rows, :] = refs[index][...]

    @pl.when(place_ref[1] % 2 == 0)
    def _():
        onward[: count * rows, :] = out[...]
        if onward.shape[0] > count * rows:
            onward[count * rows :, :] = refs[count][count * rows : onward.shape[0], :]

    @pl.when(place_ref[1] % 2 == 1)
    def _():
        onward[...] = refs[count][: onward.shape[0], :]


def stacked(pieces, place, held, after, onward_rows=0):
    rows, virs = pieces[0].shape
    count = len(pieces)
    whole = pl.BlockSpec((count * rows, virs), lambda: (0, 0))
    shape = jax.ShapeDtypeStruct((count * rows, virs), pieces[0].dtype)
    kernel = join_pass_kernel if held else join_kernel
    outs = 1 + len(held)
    wide = [pl.BlockSpec((onward_rows, virs), lambda: (0, 0))] * len(held)

    def entry(place_ref, *refs):
        kernel(count, place_ref, *refs[: count + len(held)], *refs[-outs:])

    return pl.pallas_call(
        entry,
        in_specs=[pl.BlockSpec(memory_space=pltpu.SMEM)]
        + [pl.BlockSpec((rows, virs), lambda: (0, 0))] * count
        + [pl.BlockSpec(value.shape, lambda: (0, 0)) for value in held]
        + [pl.BlockSpec(memory_space=pl.ANY)] * len(after),
        out_specs=[whole] + wide,
        out_shape=[shape] + [jax.ShapeDtypeStruct((onward_rows, virs), pieces[0].dtype)] * len(held),
        compiler_params=pltpu.CompilerParams(vmem_limit_bytes=20 * MIB),
        cost_estimate=pl.CostEstimate(flops=0, bytes_accessed=4 * count * rows * virs * outs, transcendentals=0),
        name="join",
    )(place, *pieces, *held, *after)


def pick_kernel(late, place_ref, own_ref, near_ref, late_ref, *refs):
    out = refs[-1]
    is_late = functools.reduce(jnp.logical_or, [place_ref[1] == n for n in late], place_ref[1] < 0)
    out[0] = own_ref[...]

    @pl.when(jnp.logical_not(is_late))
    def _():
        out[1] = near_ref[...]

    @pl.when(is_late)
    def _():
        out[1] = late_ref[...]


def with_next(own, near, late_near, late, place, after):
    rows, virs = own.shape
    block = rows // 2
    return pl.pallas_call(
        functools.partial(pick_kernel, late),
        grid=(rows // block,),
        in_specs=[pl.BlockSpec(memory_space=pltpu.SMEM)]
        + [pl.BlockSpec((block, virs), lambda g: (g, 0))] * 3
        + [pl.BlockSpec(memory_space=pl.ANY)] * len(after),
        out_specs=pl.BlockSpec((2, block, virs), lambda g: (0, g, 0)),
        out_shape=jax.ShapeDtypeStruct((2, rows, virs), own.dtype),
        compiler_params=pltpu.CompilerParams(vmem_limit_bytes=16 * MIB),
        cost_estimate=pl.CostEstimate(flops=0, bytes_accessed=10 * rows * virs, transcendentals=0),
        name="pick",
    )(place, own, near, late_near, *after)


def slot_orbital(place_ref, aux_count, occ_count, slot):
    block = lax.rem(place_ref[1] + slot // OCC_DEV, occ_count) * aux_count + place_ref[0]
    return block * OCC_DEV + slot % OCC_DEV


def energy_kernel(aux_count, occ_count, place_ref, dom_ref, table_ref, row_ref, col_ref):
    slots, _, virs = row_ref.shape
    lanes = table_ref.shape[1]
    rows = []
    for slot in range(slots):
        orbital = slot_orbital(place_ref, aux_count, occ_count, slot)
        rows.append(dom_ref[pl.ds(orbital, 1), :])
    doms = jnp.concatenate(rows, axis=0)
    for part in range(virs // lanes):
        span = slice(part * lanes, (part + 1) * lanes)
        dom = doms[:, span]
        high, low = dom // lanes, dom % lanes
        total = jnp.zeros((slots, lanes), jnp.float32)
        for line in range(table_ref.shape[0]):
            table = jnp.broadcast_to(table_ref[line : line + 1, :], (slots, lanes))
            found = jnp.take_along_axis(table, low, axis=1, mode="promise_in_bounds")
            total = jnp.where(high == line, found, total)
        row_ref[:, 0, span] = total
        col_ref[span, :] = total.T


def energies(place, domains, vir_energy, aux_count, occ_count):
    slots, virs = PARTNERS * OCC_DEV, domains.shape[1]
    vmem = pl.BlockSpec(memory_space=pltpu.VMEM)
    return pl.pallas_call(
        functools.partial(energy_kernel, aux_count, occ_count),
        in_specs=[pl.BlockSpec(memory_space=pltpu.SMEM), vmem, vmem],
        out_specs=[vmem, vmem],
        out_shape=[
            jax.ShapeDtypeStruct((slots, 1, virs), jnp.float32),
            jax.ShapeDtypeStruct((virs, slots), jnp.float32),
        ],
        compiler_params=pltpu.CompilerParams(vmem_limit_bytes=8 * MIB),
        cost_estimate=pl.CostEstimate(flops=0, bytes_accessed=4 * domains.size, transcendentals=0),
        name="energies",
    )(place, domains, vir_energy.reshape(-1, 128))


def pair_kernel(chunk, count, occ_count, live_ref, code_ref, place_ref, occ_ref, *refs):
    own_refs, (col_ref, row_ref), refs = refs[:count], refs[count : count + 2], refs[count + 2 :]
    sets = 3
    blocks = refs[: sets * OCC_DEV]
    outs = refs[sets * OCC_DEV : sets * OCC_DEV + count]
    turned, total, held, sems, todo = refs[sets * OCC_DEV + count :]
    split = own_refs[0].shape[0]
    aux = split * count
    span = PARTNERS * OCC_DEV
    slots = code_ref.shape[0]
    odd = place_ref[1] % 2

    def scan(slot, found):
        code = code_ref[slot]
        mine = (slot < live_ref[0, 0]) & (code // span == chunk)

        @pl.when(mine)
        def _():
            todo[found] = code % span

        return found + mine.astype(jnp.int32)

    pairs = lax.fori_loop(0, slots, scan, jnp.int32(0))

    def source(slot):
        offset = slot // OCC_DEV
        one = jnp.where(odd == 1, 3, 2)
        three = jnp.where(odd == 1, 4, 3)
        kind = jnp.where(offset == 0, 0, jnp.where(offset == 1, one, jnp.where(offset == 2, 1, three)))
        return kind * OCC_DEV + slot % OCC_DEV

    def fetch(index):
        place = source(todo[index])
        buffer = lax.rem(index, 2)
        for kind in range(5):
            parts = [blocks[kind // 2 * OCC_DEV + orbital] for orbital in range(OCC_DEV)]
            parts = [part.at[kind % 2] for part in parts] if kind < 4 else parts
            for orbital in range(OCC_DEV):
                @pl.when(place == kind * OCC_DEV + orbital)
                def _():
                    if orbital == 0:
                        first, rest = parts[0].at[pl.ds(0, split)], parts[0].at[pl.ds(split, aux - split)]
                    else:
                        start = aux if orbital == 1 else aux - split
                        first = parts[orbital - 1].at[pl.ds(start, split)]
                        rest = parts[orbital].at[pl.ds(0, aux - split)]
                    pltpu.make_async_copy(first, held.at[buffer, pl.ds(0, split)], sems.at[buffer, 0]).start()
                    pltpu.make_async_copy(rest, held.at[buffer, pl.ds(split, aux - split)], sems.at[buffer, 1]).start()

    @pl.when(pairs > 0)
    def _():
        fetch(0)
        for index, own_ref in enumerate(own_refs):
            turned[:, index * split : (index + 1) * split] = own_ref[...].T

    total[...] = jnp.zeros_like(total)

    def step(index, carry):
        @pl.when(index + 1 < pairs)
        def _():
            fetch(index + 1)

        buffer = lax.rem(index, 2)
        first, rest = held.at[buffer, pl.ds(0, split)], held.at[buffer, pl.ds(split, aux - split)]
        pltpu.make_async_copy(blocks[0].at[0, pl.ds(0, split)], first, sems.at[buffer, 0]).wait()
        pltpu.make_async_copy(blocks[0].at[0, pl.ds(split, aux - split)], rest, sems.at[buffer, 1]).wait()
        slot = todo[index]
        energy = lambda which: occ_ref[slot_orbital(place_ref, count, occ_count, which)]
        shift = energy(chunk) + energy(slot)
        other = held[buffer]
        exchange = jnp.dot(turned[...], other, preferred_element_type=jnp.float32)
        denom = (col_ref[:, chunk : chunk + 1] + row_ref[slot]) - shift
        amplitude = (exchange / denom).astype(jnp.bfloat16)
        total[...] += lax.dot_general(
            other, amplitude, (((1,), (1,)), ((), ())), preferred_element_type=jnp.float32
        )
        return carry

    lax.fori_loop(0, pairs, step, jnp.int32(0))
    part = outs[0].shape[0]
    for index, out in enumerate(outs):
        out[...] = total[index * part : (index + 1) * part, :].astype(jnp.bfloat16)


def densities(chunk, count, occ_count, live, codes, place, occ_energy, own, own_vir, vir_rows, blocks):
    rows, virs = own[0].shape
    aux = rows * count
    whole = lambda shape: pl.BlockSpec(shape, lambda: (0,) * len(shape))
    smem = pl.BlockSpec(memory_space=pltpu.SMEM)
    return pl.pallas_call(
        functools.partial(pair_kernel, chunk, count, occ_count),
        in_specs=[smem] * 4 + [whole((rows, virs))] * count + [whole(own_vir.shape), whole(vir_rows.shape)]
        + [pl.BlockSpec(memory_space=pl.ANY)] * len(blocks),
        out_specs=[whole((rows, virs))] * count,
        out_shape=[jax.ShapeDtypeStruct((rows, virs), jnp.bfloat16)] * count,
        scratch_shapes=[
            pltpu.VMEM((virs, aux), jnp.bfloat16),
            pltpu.VMEM((aux, virs), jnp.float32),
            pltpu.VMEM((2, aux, virs), jnp.bfloat16),
            pltpu.SemaphoreType.DMA((2, 2)),
            pltpu.SMEM((codes.shape[0],), jnp.int32),
        ],
        compiler_params=pltpu.CompilerParams(vmem_limit_bytes=20 * MIB),
        cost_estimate=pl.CostEstimate(
            flops=4 * 4 * aux * virs * virs, bytes_accessed=6 * aux * virs, transcendentals=0
        ),
        name="pairs",
    )(live, codes, place, occ_energy, *own, own_vir, vir_rows, *blocks)


def spread_kernel(count, pos_ref, *refs):
    pieces, out = refs[:-1], refs[-1]
    orbitals = count * OCC_DEV
    width = orbitals * ROWS
    row = lax.broadcasted_iota(jnp.int32, (width, width), 0)
    col = lax.broadcasted_iota(jnp.int32, (width, width), 1)
    group = col // ROWS
    place = lax.rem(pos_ref[0] + group % count, count) * OCC_DEV + group // count
    hit = jnp.where((row % orbitals == place) & (row // orbitals == col % ROWS), 1.0, 0.0).astype(jnp.bfloat16)
    for part in range(out.shape[0] // ROWS):
        span = pl.ds(part * ROWS, ROWS)
        rows = jnp.concatenate([piece[span, :] for piece in pieces], axis=0)
        moved = jnp.dot(hit, rows, preferred_element_type=jnp.float32).astype(jnp.bfloat16)
        out[span] = moved.reshape(ROWS, orbitals, -1)


def assembled(pieces, aux_pos, count):
    rows, virs = pieces[0].shape
    orbitals = count * OCC_DEV
    block = 4 * ROWS
    return pl.pallas_call(
        functools.partial(spread_kernel, count),
        grid_spec=pltpu.PrefetchScalarGridSpec(
            num_scalar_prefetch=1,
            grid=(rows // block,),
            in_specs=[pl.BlockSpec((block, virs), lambda g, pos: (g, 0))] * len(pieces),
            out_specs=pl.BlockSpec((block, orbitals, virs), lambda g, pos: (g, 0, 0)),
        ),
        out_shape=jax.ShapeDtypeStruct((rows, orbitals, virs), jnp.bfloat16),
        compiler_params=pltpu.CompilerParams(vmem_limit_bytes=20 * MIB),
        cost_estimate=pl.CostEstimate(
            flops=2 * rows * orbitals * virs * orbitals * ROWS,
            bytes_accessed=4 * rows * orbitals * virs,
            transcendentals=0,
        ),
        name="assemble",
    )(aux_pos, *pieces)


def body(half_ints, block_mask, vir_coef, domains, vir_energy, occ_energy, pair_count, pair_code):
    aux_count = lax.axis_size("aux")
    occ_count = lax.axis_size("occ")
    aux_pos = lax.axis_index("aux")
    occ_pos = lax.axis_index("occ")

    def along_aux(value, steps):
        return lax.ppermute(value, "aux", [(z, (z + steps) % aux_count) for z in range(aux_count)])

    rows_of, place = sorted_rows(
        half_ints, block_mask, aux_pos.astype(jnp.int32).reshape(1), occ_pos.astype(jnp.int32).reshape(1)
    )
    vir_rows, vir_cols = energies(place, domains, vir_energy, aux_count, occ_count)
    twin, direct, far, last, late = routes(occ_count)
    transform = functools.partial(transformed, rows_of, domains, vir_coef, place, aux_count)

    order = list(range(1, aux_count)) + [0]
    sent = [None] * aux_count
    for step in order:
        sent[step] = transform(0, 0, step, 0, 1, [])[0]
    pieces = [sent[0]] + [along_aux(sent[step], step) for step in range(1, aux_count)]
    parts, owns, nears, thirds, lates, sets, swaps = [], [], [], [], [], [], []
    after = [sent[0]]
    for chunk in range(OCC_DEV + 1):
        coming = []
        if chunk + 1 < OCC_DEV:
            sent = transform(chunk + 1, 0, 0, 1, aux_count, after)
            coming = [sent[0]] + [along_aux(sent[step], step) for step in range(1, aux_count)]
        if chunk < OCC_DEV:
            parts.append(pieces)
            message = pieces[0 if chunk == 0 else 1 :] + coming[:1]
            rides = bool(last) and 0 < chunk < OCC_DEV - 1
            ready = nears[-1:] + ([] if rides else thirds[-1:])
            onward_rows = max(sum(piece.shape[0] for piece in message), owns[-1].shape[0]) if rides else 0
            own, *onward = stacked(message, place, thirds[-1:] if rides else [], ready, onward_rows)
            near = lax.ppermute(own, "occ", direct)
            third = lax.ppermute(onward[0], "occ", far + last) if rides else lax.ppermute(own, "occ", far)
            owns.append(own)
            nears.append(near)
            thirds.append(third)
            if rides:
                lates.append(third)
            if last and chunk >= OCC_DEV - 2:
                lates.append(lax.ppermute(third, "occ", last))
            if not last:
                lates.append(near)
        if chunk >= 1:
            waits = coming[1:] + nears[-1:] if coming else []
            both = with_next(owns[chunk - 1], nears[chunk - 1], lates[chunk - 1], late, place, waits)
            sets.append(both)
            swaps.append(lax.ppermute(both, "occ", twin))
        pieces, after = coming, [own, vir_rows]
    blocks = sets + swaps + thirds
    codes = pair_code[0, 0]
    results = []
    for chunk in range(OCC_DEV):
        pieces = densities(
            chunk, aux_count, occ_count, pair_count, codes, place, occ_energy, parts[chunk], vir_cols, vir_rows, blocks
        )
        results += [pieces[0]] + [along_aux(pieces[step], -step) for step in range(1, aux_count)]
    return assembled(results, place, aux_count)


def routes(count):
    chips = count // 2
    twin = [(n, n ^ 1) for n in range(count)]
    turned = [c for c in range(0, chips, 2)] if chips == 4 else []
    direct = [(n, (n - 2) % count) for n in range(count) if n % 2 or n // 2 not in turned]
    far = [((n + 3) % count, n) for n in range(1, count, 2)]
    last = [(2 * ((c + 2) % chips) + 1, 2 * ((c - 1) % chips)) for c in turned]
    late = [target for _, target in last]
    return twin, direct, far, last, late


def solution(mesh):
    placed = (
        P("aux", "occ", None),
        P("aux", "occ"),
        P(),
        P(),
        P(),
        P(),
        P("occ", "aux"),
        P("occ", "aux", None),
    )
    return jax.shard_map(
        body, mesh=mesh, in_specs=placed, out_specs=P("aux", "occ", None), check_vma=False
    )
```

```python
import functools

import jax
import jax.numpy as jnp
from jax import lax
from jax.experimental import pallas as pl
from jax.experimental.pallas import tpu as pltpu
from jax.sharding import PartitionSpec as P

BLK = 64
OCC_DEV = 4
PARTNERS = 4
ROWS = 16
MIB = 1024 * 1024


def sort_kernel(mask_ref, aux_ref, occ_ref, x_ref, out_ref, place_ref):
    step = pl.program_id(0)
    block, orbitals, basis = x_ref.shape
    width = orbitals * ROWS
    place_ref[0] = aux_ref[0]
    place_ref[1] = occ_ref[0]
    row = lax.broadcasted_iota(jnp.int32, (ROWS, width), 0)
    col = lax.broadcasted_iota(jnp.int32, (ROWS, width), 1)
    spread = jnp.concatenate(
        [
            jnp.where(
                col == row * orbitals + orbital, mask_ref[step * block // BLK, orbital].astype(jnp.float32), 0.0
            )
            for orbital in range(orbitals)
        ],
        axis=0,
    ).astype(jnp.bfloat16)
    for part in range(block // ROWS):
        span = slice(part * ROWS, (part + 1) * ROWS)
        moved = jnp.dot(spread, x_ref[span].reshape(width, basis), preferred_element_type=jnp.float32)
        out_ref[:, span, :] = moved.astype(jnp.bfloat16).reshape(orbitals, ROWS, basis)


def sorted_rows(half_ints, block_mask, aux_pos, occ_pos):
    rows, orbitals, basis = half_ints.shape
    block = BLK
    smem = pl.BlockSpec(memory_space=pltpu.SMEM)
    return pl.pallas_call(
        sort_kernel,
        grid=(rows // block,),
        in_specs=[
            smem,
            smem,
            smem,
            pl.BlockSpec((block, orbitals, basis), lambda g: (g, 0, 0)),
        ],
        out_specs=[
            pl.BlockSpec((orbitals, block, basis), lambda g: (0, g, 0)),
            smem,
        ],
        out_shape=[
            jax.ShapeDtypeStruct((orbitals, rows, basis), jnp.bfloat16),
            jax.ShapeDtypeStruct((2,), jnp.int32),
        ],
        compiler_params=pltpu.CompilerParams(vmem_limit_bytes=40 * MIB),
        cost_estimate=pl.CostEstimate(
            flops=2 * rows * orbitals * basis * orbitals * ROWS,
            bytes_accessed=4 * rows * orbitals * basis,
            transcendentals=0,
        ),
        name="sort_rows",
    )(block_mask, aux_pos, occ_pos, half_ints)


def transform_kernel(count, orbitals, orbital, after, pos_ref, x_ref, dom_ref, coef_ref, *refs):
    out_refs = refs[after:]
    step = pl.program_id(0)
    tile = 512
    whole = coef_ref.shape[1]
    dom = dom_ref[pl.ds(pos_ref[1] * orbitals + orbital(step, pos_ref), 1), :]
    total = None
    for part in range(whole // tile):
        full = jnp.dot(
            x_ref[...], coef_ref[:, part * tile : (part + 1) * tile], preferred_element_type=jnp.float32
        ).astype(jnp.bfloat16)
        row = lax.broadcasted_iota(jnp.int32, (tile, dom.shape[1]), 0) + part * tile
        pick = jnp.where(row == dom, 1.0, 0.0).astype(jnp.bfloat16)
        term = jnp.dot(full, pick, preferred_element_type=jnp.float32)
        total = term if total is None else total + term
    total = total.astype(jnp.bfloat16)
    for index in range(count):
        @pl.when(step == index)
        def _():
            out_refs[index][...] = total


def transformed(rows_of, domains, vir_coef, place, aux_count, chunk, chunk_step, first, first_step, count, after):
    orbitals, rows, basis = rows_of.shape
    virs = domains.shape[1]
    whole = vir_coef.shape[1]

    def orbital(step, pos_ref):
        return lax.rem(pos_ref[0] + first + step * first_step, aux_count) * OCC_DEV + chunk + step * chunk_step

    return pl.pallas_call(
        functools.partial(transform_kernel, count, orbitals, orbital, len(after)),
        grid_spec=pltpu.PrefetchScalarGridSpec(
            num_scalar_prefetch=1,
            grid=(count,),
            in_specs=[
                pl.BlockSpec((None, rows, basis), lambda g, pos: (orbital(g, pos), 0, 0)),
                pl.BlockSpec(domains.shape, lambda g, pos: (0, 0)),
                pl.BlockSpec((basis, whole), lambda g, pos: (0, 0), pipeline_mode=pl.Buffered(1)),
            ]
            + [pl.BlockSpec(memory_space=pl.ANY)] * len(after),
            out_specs=[pl.BlockSpec((rows, virs), lambda g, pos: (0, 0)) for _ in range(count)],
        ),
        out_shape=[jax.ShapeDtypeStruct((rows, virs), jnp.bfloat16) for _ in range(count)],
        compiler_params=pltpu.CompilerParams(vmem_limit_bytes=20 * MIB),
        cost_estimate=pl.CostEstimate(
            flops=2 * count * rows * whole * (basis + virs),
            bytes_accessed=2 * (count * rows * (basis + virs) + basis * whole),
            transcendentals=0,
        ),
        name="transform",
    )(place, rows_of, domains, vir_coef, *after)


def join_kernel(count, place_ref, *refs):
    out = refs[count]
    rows = refs[0].shape[0]
    for index in range(count):
        out[index * rows : (index + 1) * rows, :] = refs[index][...]


def join_pass_kernel(count, place_ref, *refs):
    out, onward = refs[-2:]
    rows = refs[0].shape[0]
    for index in range(count):
        out[index * rows : (index + 1) * rows, :] = refs[index][...]

    @pl.when(place_ref[1] % 2 == 0)
    def _():
        onward[: count * rows, :] = out[...]
        if onward.shape[0] > count * rows:
            onward[count * rows :, :] = refs[count][count * rows : onward.shape[0], :]

    @pl.when(place_ref[1] % 2 == 1)
    def _():
        known = min(onward.shape[0], refs[count].shape[0])
        onward[:known, :] = refs[count][:known, :]
        if onward.shape[0] > known:
            onward[known:, :] = out[known : onward.shape[0], :]


def stacked(pieces, place, held, after, onward_rows=0):
    rows, virs = pieces[0].shape
    count = len(pieces)
    whole = pl.BlockSpec((count * rows, virs), lambda: (0, 0))
    shape = jax.ShapeDtypeStruct((count * rows, virs), pieces[0].dtype)
    kernel = join_pass_kernel if held else join_kernel
    outs = 1 + len(held)
    wide = [pl.BlockSpec((onward_rows, virs), lambda: (0, 0))] * len(held)

    def entry(place_ref, *refs):
        kernel(count, place_ref, *refs[: count + len(held)], *refs[-outs:])

    return pl.pallas_call(
        entry,
        in_specs=[pl.BlockSpec(memory_space=pltpu.SMEM)]
        + [pl.BlockSpec((rows, virs), lambda: (0, 0))] * count
        + [pl.BlockSpec(value.shape, lambda: (0, 0)) for value in held]
        + [pl.BlockSpec(memory_space=pl.ANY)] * len(after),
        out_specs=[whole] + wide,
        out_shape=[shape] + [jax.ShapeDtypeStruct((onward_rows, virs), pieces[0].dtype)] * len(held),
        compiler_params=pltpu.CompilerParams(vmem_limit_bytes=20 * MIB),
        cost_estimate=pl.CostEstimate(flops=0, bytes_accessed=4 * count * rows * virs * outs, transcendentals=0),
        name="join",
    )(place, *pieces, *held, *after)


def pick_kernel(late, place_ref, own_ref, near_ref, late_ref, *refs):
    out = refs[-1]
    is_late = functools.reduce(jnp.logical_or, [place_ref[1] == n for n in late], place_ref[1] < 0)
    out[0] = own_ref[...]

    @pl.when(jnp.logical_not(is_late))
    def _():
        out[1] = near_ref[...]

    @pl.when(is_late)
    def _():
        out[1] = late_ref[...]


def with_next(own, near, late_near, late, place, after):
    rows, virs = own.shape
    block = rows // 2
    return pl.pallas_call(
        functools.partial(pick_kernel, late),
        grid=(rows // block,),
        in_specs=[pl.BlockSpec(memory_space=pltpu.SMEM)]
        + [pl.BlockSpec((block, virs), lambda g: (g, 0))] * 3
        + [pl.BlockSpec(memory_space=pl.ANY)] * len(after),
        out_specs=pl.BlockSpec((2, block, virs), lambda g: (0, g, 0)),
        out_shape=jax.ShapeDtypeStruct((2, rows, virs), own.dtype),
        compiler_params=pltpu.CompilerParams(vmem_limit_bytes=16 * MIB),
        cost_estimate=pl.CostEstimate(flops=0, bytes_accessed=10 * rows * virs, transcendentals=0),
        name="pick",
    )(place, own, near, late_near, *after)


def slot_orbital(place_ref, aux_count, occ_count, slot):
    block = lax.rem(place_ref[1] + slot // OCC_DEV, occ_count) * aux_count + place_ref[0]
    return block * OCC_DEV + slot % OCC_DEV


def energy_kernel(aux_count, occ_count, place_ref, dom_ref, table_ref, row_ref, col_ref):
    slots, _, virs = row_ref.shape
    lanes = table_ref.shape[1]
    rows = []
    for slot in range(slots):
        orbital = slot_orbital(place_ref, aux_count, occ_count, slot)
        rows.append(dom_ref[pl.ds(orbital, 1), :])
    doms = jnp.concatenate(rows, axis=0)
    for part in range(virs // lanes):
        span = slice(part * lanes, (part + 1) * lanes)
        dom = doms[:, span]
        high, low = dom // lanes, dom % lanes
        total = jnp.zeros((slots, lanes), jnp.float32)
        for line in range(table_ref.shape[0]):
            table = jnp.broadcast_to(table_ref[line : line + 1, :], (slots, lanes))
            found = jnp.take_along_axis(table, low, axis=1, mode="promise_in_bounds")
            total = jnp.where(high == line, found, total)
        row_ref[:, 0, span] = total
        col_ref[span, :] = total.T


def energies(place, domains, vir_energy, aux_count, occ_count):
    slots, virs = PARTNERS * OCC_DEV, domains.shape[1]
    vmem = pl.BlockSpec(memory_space=pltpu.VMEM)
    return pl.pallas_call(
        functools.partial(energy_kernel, aux_count, occ_count),
        in_specs=[pl.BlockSpec(memory_space=pltpu.SMEM), vmem, vmem],
        out_specs=[vmem, vmem],
        out_shape=[
            jax.ShapeDtypeStruct((slots, 1, virs), jnp.float32),
            jax.ShapeDtypeStruct((virs, slots), jnp.float32),
        ],
        compiler_params=pltpu.CompilerParams(vmem_limit_bytes=8 * MIB),
        cost_estimate=pl.CostEstimate(flops=0, bytes_accessed=4 * domains.size, transcendentals=0),
        name="energies",
    )(place, domains, vir_energy.reshape(-1, 128))


def pair_kernel(chunk, count, occ_count, live_ref, code_ref, place_ref, occ_ref, *refs):
    own_refs, (col_ref, row_ref), refs = refs[:count], refs[count : count + 2], refs[count + 2 :]
    sets = 3
    blocks = refs[: sets * OCC_DEV]
    outs = refs[sets * OCC_DEV : sets * OCC_DEV + count]
    turned, total, held, sems, todo = refs[sets * OCC_DEV + count :]
    split = own_refs[0].shape[0]
    aux = split * count
    span = PARTNERS * OCC_DEV
    slots = code_ref.shape[0]
    odd = place_ref[1] % 2

    def scan(slot, found):
        code = code_ref[slot]
        mine = (slot < live_ref[0, 0]) & (code // span == chunk)

        @pl.when(mine)
        def _():
            todo[found] = code % span

        return found + mine.astype(jnp.int32)

    pairs = lax.fori_loop(0, slots, scan, jnp.int32(0))

    def source(slot):
        offset = slot // OCC_DEV
        one = jnp.where(odd == 1, 3, 2)
        three = jnp.where(odd == 1, 4, 3)
        kind = jnp.where(offset == 0, 0, jnp.where(offset == 1, one, jnp.where(offset == 2, 1, three)))
        return kind * OCC_DEV + slot % OCC_DEV

    def fetch(index):
        place = source(todo[index])
        buffer = lax.rem(index, 2)
        for kind in range(5):
            parts = [blocks[kind // 2 * OCC_DEV + orbital] for orbital in range(OCC_DEV)]
            parts = [part.at[kind % 2] for part in parts] if kind < 4 else parts
            for orbital in range(OCC_DEV):
                @pl.when(place == kind * OCC_DEV + orbital)
                def _():
                    if orbital <= 1:
                        first, rest = (parts[orbital].at[pl.ds(start, size)] for start, size in ((0, split), (split, aux - split)))
                    else:
                        start = aux if orbital == 2 else aux - split
                        first = parts[orbital - 1].at[pl.ds(start, split)]
                        rest = parts[orbital].at[pl.ds(0, aux - split)]
                    pltpu.make_async_copy(first, held.at[buffer, pl.ds(0, split)], sems.at[buffer, 0]).start()
                    pltpu.make_async_copy(rest, held.at[buffer, pl.ds(split, aux - split)], sems.at[buffer, 1]).start()

    @pl.when(pairs > 0)
    def _():
        fetch(0)
        for index, own_ref in enumerate(own_refs):
            turned[:, index * split : (index + 1) * split] = own_ref[...].T

    total[...] = jnp.zeros_like(total)

    def step(index, carry):
        @pl.when(index + 1 < pairs)
        def _():
            fetch(index + 1)

        buffer = lax.rem(index, 2)
        first, rest = held.at[buffer, pl.ds(0, split)], held.at[buffer, pl.ds(split, aux - split)]
        pltpu.make_async_copy(blocks[0].at[0, pl.ds(0, split)], first, sems.at[buffer, 0]).wait()
        pltpu.make_async_copy(blocks[0].at[0, pl.ds(split, aux - split)], rest, sems.at[buffer, 1]).wait()
        slot = todo[index]
        energy = lambda which: occ_ref[slot_orbital(place_ref, count, occ_count, which)]
        shift = energy(chunk) + energy(slot)
        other = held[buffer]
        half = turned.shape[0] // 2
        halves = [slice(0, half), slice(half, 2 * half)]
        exchanges = [jnp.dot(turned[span, :], other, preferred_element_type=jnp.float32) for span in halves]
        for span, exchange in zip(halves, exchanges):
            denom = (col_ref[span, chunk : chunk + 1] + row_ref[slot]) - shift
            amplitude = (exchange / denom).astype(jnp.bfloat16)
            total[:, span] += lax.dot_general(
                other, amplitude, (((1,), (1,)), ((), ())), preferred_element_type=jnp.float32
            )
        return carry

    lax.fori_loop(0, pairs, step, jnp.int32(0))
    part = outs[0].shape[0]
    for index, out in enumerate(outs):
        out[...] = total[index * part : (index + 1) * part, :].astype(jnp.bfloat16)


def densities(chunk, count, occ_count, live, codes, place, occ_energy, own, own_vir, vir_rows, blocks):
    rows, virs = own[0].shape
    aux = rows * count
    whole = lambda shape: pl.BlockSpec(shape, lambda: (0,) * len(shape))
    smem = pl.BlockSpec(memory_space=pltpu.SMEM)
    return pl.pallas_call(
        functools.partial(pair_kernel, chunk, count, occ_count),
        in_specs=[smem] * 4 + [whole((rows, virs))] * count + [whole(own_vir.shape), whole(vir_rows.shape)]
        + [pl.BlockSpec(memory_space=pl.ANY)] * len(blocks),
        out_specs=[whole((rows, virs))] * count,
        out_shape=[jax.ShapeDtypeStruct((rows, virs), jnp.bfloat16)] * count,
        scratch_shapes=[
            pltpu.VMEM((virs, aux), jnp.bfloat16),
            pltpu.VMEM((aux, virs), jnp.float32),
            pltpu.VMEM((2, aux, virs), jnp.bfloat16),
            pltpu.SemaphoreType.DMA((2, 2)),
            pltpu.SMEM((codes.shape[0],), jnp.int32),
        ],
        compiler_params=pltpu.CompilerParams(vmem_limit_bytes=20 * MIB),
        cost_estimate=pl.CostEstimate(
            flops=4 * 4 * aux * virs * virs, bytes_accessed=6 * aux * virs, transcendentals=0
        ),
        name="pairs",
    )(live, codes, place, occ_energy, *own, own_vir, vir_rows, *blocks)


def spread_kernel(count, pos_ref, *refs):
    pieces, out = refs[:-1], refs[-1]
    orbitals = count * OCC_DEV
    width = orbitals * ROWS
    row = lax.broadcasted_iota(jnp.int32, (width, width), 0)
    col = lax.broadcasted_iota(jnp.int32, (width, width), 1)
    group = col // ROWS
    place = lax.rem(pos_ref[0] + group % count, count) * OCC_DEV + group // count
    hit = jnp.where((row % orbitals == place) & (row // orbitals == col % ROWS), 1.0, 0.0).astype(jnp.bfloat16)
    for part in range(out.shape[0] // ROWS):
        span = pl.ds(part * ROWS, ROWS)
        rows = jnp.concatenate([piece[span, :] for piece in pieces], axis=0)
        moved = jnp.dot(hit, rows, preferred_element_type=jnp.float32).astype(jnp.bfloat16)
        out[span] = moved.reshape(ROWS, orbitals, -1)


def assembled(pieces, aux_pos, count):
    rows, virs = pieces[0].shape
    orbitals = count * OCC_DEV
    block = 4 * ROWS
    return pl.pallas_call(
        functools.partial(spread_kernel, count),
        grid_spec=pltpu.PrefetchScalarGridSpec(
            num_scalar_prefetch=1,
            grid=(rows // block,),
            in_specs=[pl.BlockSpec((block, virs), lambda g, pos: (g, 0))] * len(pieces),
            out_specs=pl.BlockSpec((block, orbitals, virs), lambda g, pos: (g, 0, 0)),
        ),
        out_shape=jax.ShapeDtypeStruct((rows, orbitals, virs), jnp.bfloat16),
        compiler_params=pltpu.CompilerParams(vmem_limit_bytes=20 * MIB),
        cost_estimate=pl.CostEstimate(
            flops=2 * rows * orbitals * virs * orbitals * ROWS,
            bytes_accessed=4 * rows * orbitals * virs,
            transcendentals=0,
        ),
        name="assemble",
    )(aux_pos, *pieces)


def body(half_ints, block_mask, vir_coef, domains, vir_energy, occ_energy, pair_count, pair_code):
    aux_count = lax.axis_size("aux")
    occ_count = lax.axis_size("occ")
    aux_pos = lax.axis_index("aux")
    occ_pos = lax.axis_index("occ")

    def along_aux(value, steps):
        return lax.ppermute(value, "aux", [(z, (z + steps) % aux_count) for z in range(aux_count)])

    rows_of, place = sorted_rows(
        half_ints, block_mask, aux_pos.astype(jnp.int32).reshape(1), occ_pos.astype(jnp.int32).reshape(1)
    )
    vir_rows, vir_cols = energies(place, domains, vir_energy, aux_count, occ_count)
    twin, direct, far, last, late = routes(occ_count)
    transform = functools.partial(transformed, rows_of, domains, vir_coef, place, aux_count)

    order = list(range(1, aux_count)) + [0]
    sent = [None] * aux_count
    for step in order:
        sent[step] = transform(0, 0, step, 0, 1, [])[0]
    pieces = [sent[0]] + [along_aux(sent[step], step) for step in range(1, aux_count)]
    parts, owns, nears, thirds, lates, sets, swaps = [], [], [], [], [], [], []
    after = [sent[0]]
    for chunk in range(OCC_DEV + 1):
        coming = []
        if chunk + 1 < OCC_DEV:
            sent = transform(chunk + 1, 0, 0, 1, aux_count, after)
            coming = [sent[0]] + [along_aux(sent[step], step) for step in range(1, aux_count)]
        if chunk < OCC_DEV:
            parts.append(pieces)
            message = pieces[0 if chunk <= 1 else 1 :] + (coming[:1] if chunk >= 1 else [])
            rides = bool(last) and 0 < chunk < OCC_DEV - 1
            ready = nears[-1:] + ([] if rides else thirds[-1:]) + (coming[:1] if chunk == 0 else [])
            onward_rows = max(sum(piece.shape[0] for piece in message), owns[-1].shape[0]) if rides else 0
            own, *onward = stacked(message, place, thirds[-1:] if rides else [], ready, onward_rows)
            near = lax.ppermute(own, "occ", direct)
            third = lax.ppermute(onward[0], "occ", far + last) if rides else lax.ppermute(own, "occ", far)
            owns.append(own)
            nears.append(near)
            thirds.append(third)
            if rides:
                lates.append(third)
            if last and chunk >= OCC_DEV - 2:
                lates.append(lax.ppermute(third, "occ", last))
            if not last:
                lates.append(near)
        if chunk >= 1:
            waits = coming[1:] + nears[-1:] if coming else []
            both = with_next(owns[chunk - 1], nears[chunk - 1], lates[chunk - 1], late, place, waits)
            sets.append(both)
            swaps.append(lax.ppermute(both, "occ", twin))
        pieces, after = coming, [own, vir_rows]
    blocks = sets + swaps + thirds
    codes = pair_code[0, 0]
    results = []
    for chunk in range(OCC_DEV):
        pieces = densities(
            chunk, aux_count, occ_count, pair_count, codes, place, occ_energy, parts[chunk], vir_cols, vir_rows, blocks
        )
        results += [pieces[0]] + [along_aux(pieces[step], -step) for step in range(1, aux_count)]
    return assembled(results, place, aux_count)


def routes(count):
    chips = count // 2
    twin = [(n, n ^ 1) for n in range(count)]
    turned = [c for c in range(0, chips, 2)] if chips == 4 else []
    direct = [(n, (n - 2) % count) for n in range(count) if n % 2 or n // 2 not in turned]
    far = [((n + 3) % count, n) for n in range(1, count, 2)]
    last = [(2 * ((c + 2) % chips) + 1, 2 * ((c - 1) % chips)) for c in turned]
    late = [target for _, target in last]
    return twin, direct, far, last, late


def solution(mesh):
    placed = (
        P("aux", "occ", None),
        P("aux", "occ"),
        P(),
        P(),
        P(),
        P(),
        P("occ", "aux"),
        P("occ", "aux", None),
    )
    return jax.shard_map(
        body, mesh=mesh, in_specs=placed, out_specs=P("aux", "occ", None), check_vma=False
    )
```

```python
import functools

import jax
import jax.numpy as jnp
from jax import lax
from jax.experimental import pallas as pl
from jax.experimental.pallas import tpu as pltpu
from jax.sharding import PartitionSpec as P

BLK = 64
OCC_DEV = 4
PARTNERS = 4
ROWS = 16
MIB = 1024 * 1024


def sort_kernel(mask_ref, aux_ref, occ_ref, x_ref, out_ref, place_ref):
    step = pl.program_id(0)
    block, orbitals, basis = x_ref.shape
    width = orbitals * ROWS
    place_ref[0] = aux_ref[0]
    place_ref[1] = occ_ref[0]
    row = lax.broadcasted_iota(jnp.int32, (ROWS, width), 0)
    col = lax.broadcasted_iota(jnp.int32, (ROWS, width), 1)
    spread = jnp.concatenate(
        [
            jnp.where(
                col == row * orbitals + orbital, mask_ref[step * block // BLK, orbital].astype(jnp.float32), 0.0
            )
            for orbital in range(orbitals)
        ],
        axis=0,
    ).astype(jnp.bfloat16)
    for part in range(block // ROWS):
        span = slice(part * ROWS, (part + 1) * ROWS)
        moved = jnp.dot(spread, x_ref[span].reshape(width, basis), preferred_element_type=jnp.float32)
        out_ref[:, span, :] = moved.astype(jnp.bfloat16).reshape(orbitals, ROWS, basis)


def sorted_rows(half_ints, block_mask, aux_pos, occ_pos):
    rows, orbitals, basis = half_ints.shape
    block = BLK
    smem = pl.BlockSpec(memory_space=pltpu.SMEM)
    return pl.pallas_call(
        sort_kernel,
        grid=(rows // block,),
        in_specs=[
            smem,
            smem,
            smem,
            pl.BlockSpec((block, orbitals, basis), lambda g: (g, 0, 0)),
        ],
        out_specs=[
            pl.BlockSpec((orbitals, block, basis), lambda g: (0, g, 0)),
            smem,
        ],
        out_shape=[
            jax.ShapeDtypeStruct((orbitals, rows, basis), jnp.bfloat16),
            jax.ShapeDtypeStruct((2,), jnp.int32),
        ],
        compiler_params=pltpu.CompilerParams(vmem_limit_bytes=40 * MIB),
        cost_estimate=pl.CostEstimate(
            flops=2 * rows * orbitals * basis * orbitals * ROWS,
            bytes_accessed=4 * rows * orbitals * basis,
            transcendentals=0,
        ),
        name="sort_rows",
    )(block_mask, aux_pos, occ_pos, half_ints)


def transform_kernel(count, orbitals, orbital, after, pos_ref, x_ref, dom_ref, coef_ref, *refs):
    out_refs = refs[after:]
    step = pl.program_id(0)
    tile = 512
    whole = coef_ref.shape[1]
    dom = dom_ref[pl.ds(pos_ref[1] * orbitals + orbital(step, pos_ref), 1), :]
    total = None
    for part in range(whole // tile):
        full = jnp.dot(
            x_ref[...], coef_ref[:, part * tile : (part + 1) * tile], preferred_element_type=jnp.float32
        ).astype(jnp.bfloat16)
        row = lax.broadcasted_iota(jnp.int32, (tile, dom.shape[1]), 0) + part * tile
        pick = jnp.where(row == dom, 1.0, 0.0).astype(jnp.bfloat16)
        term = jnp.dot(full, pick, preferred_element_type=jnp.float32)
        total = term if total is None else total + term
    total = total.astype(jnp.bfloat16)
    for index in range(count):
        @pl.when(step == index)
        def _():
            out_refs[index][...] = total


def transformed(rows_of, domains, vir_coef, place, aux_count, chunk, chunk_step, first, first_step, count, after):
    orbitals, rows, basis = rows_of.shape
    virs = domains.shape[1]
    whole = vir_coef.shape[1]

    def orbital(step, pos_ref):
        return lax.rem(pos_ref[0] + first + step * first_step, aux_count) * OCC_DEV + chunk + step * chunk_step

    return pl.pallas_call(
        functools.partial(transform_kernel, count, orbitals, orbital, len(after)),
        grid_spec=pltpu.PrefetchScalarGridSpec(
            num_scalar_prefetch=1,
            grid=(count,),
            in_specs=[
                pl.BlockSpec((None, rows, basis), lambda g, pos: (orbital(g, pos), 0, 0)),
                pl.BlockSpec(domains.shape, lambda g, pos: (0, 0)),
                pl.BlockSpec((basis, whole), lambda g, pos: (0, 0), pipeline_mode=pl.Buffered(1)),
            ]
            + [pl.BlockSpec(memory_space=pl.ANY)] * len(after),
            out_specs=[pl.BlockSpec((rows, virs), lambda g, pos: (0, 0)) for _ in range(count)],
        ),
        out_shape=[jax.ShapeDtypeStruct((rows, virs), jnp.bfloat16) for _ in range(count)],
        compiler_params=pltpu.CompilerParams(vmem_limit_bytes=20 * MIB),
        cost_estimate=pl.CostEstimate(
            flops=2 * count * rows * whole * (basis + virs),
            bytes_accessed=2 * (count * rows * (basis + virs) + basis * whole),
            transcendentals=0,
        ),
        name="transform",
    )(place, rows_of, domains, vir_coef, *after)


def join_kernel(count, place_ref, *refs):
    out = refs[count]
    rows = refs[0].shape[0]
    for index in range(count):
        out[index * rows : (index + 1) * rows, :] = refs[index][...]


def join_pass_kernel(count, place_ref, *refs):
    out, onward = refs[-2:]
    rows = refs[0].shape[0]
    for index in range(count):
        out[index * rows : (index + 1) * rows, :] = refs[index][...]

    @pl.when(place_ref[1] % 2 == 0)
    def _():
        onward[: count * rows, :] = out[...]
        if onward.shape[0] > count * rows:
            onward[count * rows :, :] = refs[count][count * rows : onward.shape[0], :]

    @pl.when(place_ref[1] % 2 == 1)
    def _():
        known = min(onward.shape[0], refs[count].shape[0])
        onward[:known, :] = refs[count][:known, :]
        if onward.shape[0] > known:
            onward[known:, :] = out[known : onward.shape[0], :]


def stacked(pieces, place, held, after, onward_rows=0):
    rows, virs = pieces[0].shape
    count = len(pieces)
    whole = pl.BlockSpec((count * rows, virs), lambda: (0, 0))
    shape = jax.ShapeDtypeStruct((count * rows, virs), pieces[0].dtype)
    kernel = join_pass_kernel if held else join_kernel
    outs = 1 + len(held)
    wide = [pl.BlockSpec((onward_rows, virs), lambda: (0, 0))] * len(held)

    def entry(place_ref, *refs):
        kernel(count, place_ref, *refs[: count + len(held)], *refs[-outs:])

    return pl.pallas_call(
        entry,
        in_specs=[pl.BlockSpec(memory_space=pltpu.SMEM)]
        + [pl.BlockSpec((rows, virs), lambda: (0, 0))] * count
        + [pl.BlockSpec(value.shape, lambda: (0, 0)) for value in held]
        + [pl.BlockSpec(memory_space=pl.ANY)] * len(after),
        out_specs=[whole] + wide,
        out_shape=[shape] + [jax.ShapeDtypeStruct((onward_rows, virs), pieces[0].dtype)] * len(held),
        compiler_params=pltpu.CompilerParams(vmem_limit_bytes=20 * MIB),
        cost_estimate=pl.CostEstimate(flops=0, bytes_accessed=4 * count * rows * virs * outs, transcendentals=0),
        name="join",
    )(place, *pieces, *held, *after)


def pick_kernel(late, place_ref, own_ref, near_ref, late_ref, *refs):
    out = refs[-1]
    is_late = functools.reduce(jnp.logical_or, [place_ref[1] == n for n in late], place_ref[1] < 0)
    out[0] = own_ref[...]

    @pl.when(jnp.logical_not(is_late))
    def _():
        out[1] = near_ref[...]

    @pl.when(is_late)
    def _():
        out[1] = late_ref[...]


def with_next(own, near, late_near, late, place, after):
    rows, virs = own.shape
    block = rows // 2
    return pl.pallas_call(
        functools.partial(pick_kernel, late),
        grid=(rows // block,),
        in_specs=[pl.BlockSpec(memory_space=pltpu.SMEM)]
        + [pl.BlockSpec((block, virs), lambda g: (g, 0))] * 3
        + [pl.BlockSpec(memory_space=pl.ANY)] * len(after),
        out_specs=pl.BlockSpec((2, block, virs), lambda g: (0, g, 0)),
        out_shape=jax.ShapeDtypeStruct((2, rows, virs), own.dtype),
        compiler_params=pltpu.CompilerParams(vmem_limit_bytes=16 * MIB),
        cost_estimate=pl.CostEstimate(flops=0, bytes_accessed=10 * rows * virs, transcendentals=0),
        name="pick",
    )(place, own, near, late_near, *after)


def slot_orbital(place_ref, aux_count, occ_count, slot):
    block = lax.rem(place_ref[1] + slot // OCC_DEV, occ_count) * aux_count + place_ref[0]
    return block * OCC_DEV + slot % OCC_DEV


def energy_kernel(aux_count, occ_count, place_ref, dom_ref, table_ref, row_ref, col_ref):
    slots, _, virs = row_ref.shape
    lanes = table_ref.shape[1]
    rows = []
    for slot in range(slots):
        orbital = slot_orbital(place_ref, aux_count, occ_count, slot)
        rows.append(dom_ref[pl.ds(orbital, 1), :])
    doms = jnp.concatenate(rows, axis=0)
    for part in range(virs // lanes):
        span = slice(part * lanes, (part + 1) * lanes)
        dom = doms[:, span]
        high, low = dom // lanes, dom % lanes
        total = jnp.zeros((slots, lanes), jnp.float32)
        for line in range(table_ref.shape[0]):
            table = jnp.broadcast_to(table_ref[line : line + 1, :], (slots, lanes))
            found = jnp.take_along_axis(table, low, axis=1, mode="promise_in_bounds")
            total = jnp.where(high == line, found, total)
        row_ref[:, 0, span] = total
        col_ref[span, :] = total.T


def energies(place, domains, vir_energy, aux_count, occ_count):
    slots, virs = PARTNERS * OCC_DEV, domains.shape[1]
    vmem = pl.BlockSpec(memory_space=pltpu.VMEM)
    return pl.pallas_call(
        functools.partial(energy_kernel, aux_count, occ_count),
        in_specs=[pl.BlockSpec(memory_space=pltpu.SMEM), vmem, vmem],
        out_specs=[vmem, vmem],
        out_shape=[
            jax.ShapeDtypeStruct((slots, 1, virs), jnp.float32),
            jax.ShapeDtypeStruct((virs, slots), jnp.float32),
        ],
        compiler_params=pltpu.CompilerParams(vmem_limit_bytes=8 * MIB),
        cost_estimate=pl.CostEstimate(flops=0, bytes_accessed=4 * domains.size, transcendentals=0),
        name="energies",
    )(place, domains, vir_energy.reshape(-1, 128))


def ranked(code_at, live, slots):
    span = PARTNERS * OCC_DEV

    def tally(slot, counts):
        own = code_at(slot) // span
        return tuple(
            count + ((own == orbital) & (slot < live)).astype(jnp.int32) for orbital, count in enumerate(counts)
        )

    counts = lax.fori_loop(0, slots, tally, (jnp.int32(0),) * OCC_DEV)
    places = []
    for orbital, count in enumerate(counts):
        place = jnp.int32(0)
        for other, value in enumerate(counts):
            ahead = (value < count) | (value == count) if other < orbital else value < count
            place += ahead.astype(jnp.int32)
        places.append(place)
    return [
        sum(jnp.where(place == rank, orbital, 0) for orbital, place in enumerate(places)) for rank in range(OCC_DEV)
    ]


def pair_kernel(rank, count, occ_count, live_ref, code_ref, place_ref, occ_ref, col_ref, row_ref, *refs):
    sets = 3
    blocks = refs[: sets * OCC_DEV]
    outs = refs[sets * OCC_DEV : sets * OCC_DEV + count]
    turned, total, held, sems, todo = refs[sets * OCC_DEV + count :]
    aux = held.shape[1]
    split = aux // count
    span = PARTNERS * OCC_DEV
    slots = code_ref.shape[0]
    odd = place_ref[1] % 2
    own = ranked(lambda slot: code_ref[slot], live_ref[0, 0], slots)[rank]

    def scan(slot, found):
        code = code_ref[slot]
        mine = (slot < live_ref[0, 0]) & (code // span == own)

        @pl.when(mine)
        def _():
            todo[found] = code % span

        return found + mine.astype(jnp.int32)

    pairs = lax.fori_loop(0, slots, scan, jnp.int32(0))

    def source(slot):
        offset = slot // OCC_DEV
        one = jnp.where(odd == 1, 3, 2)
        three = jnp.where(odd == 1, 4, 3)
        kind = jnp.where(offset == 0, 0, jnp.where(offset == 1, one, jnp.where(offset == 2, 1, three)))
        return kind * OCC_DEV + slot % OCC_DEV

    def fetch(slot, buffer):
        place = source(slot)
        for kind in range(5):
            parts = [blocks[kind // 2 * OCC_DEV + orbital] for orbital in range(OCC_DEV)]
            parts = [part.at[kind % 2] for part in parts] if kind < 4 else parts
            for orbital in range(OCC_DEV):
                @pl.when(place == kind * OCC_DEV + orbital)
                def _():
                    if orbital <= 1:
                        first, rest = (parts[orbital].at[pl.ds(start, size)] for start, size in ((0, split), (split, aux - split)))
                    else:
                        start = aux if orbital == 2 else aux - split
                        first = parts[orbital - 1].at[pl.ds(start, split)]
                        rest = parts[orbital].at[pl.ds(0, aux - split)]
                    pltpu.make_async_copy(first, held.at[buffer, pl.ds(0, split)], sems.at[buffer, 0]).start()
                    pltpu.make_async_copy(rest, held.at[buffer, pl.ds(split, aux - split)], sems.at[buffer, 1]).start()

    def arrived(buffer):
        first, rest = held.at[buffer, pl.ds(0, split)], held.at[buffer, pl.ds(split, aux - split)]
        pltpu.make_async_copy(blocks[0].at[0, pl.ds(0, split)], first, sems.at[buffer, 0]).wait()
        pltpu.make_async_copy(blocks[0].at[0, pl.ds(split, aux - split)], rest, sems.at[buffer, 1]).wait()

    @pl.when(pairs > 0)
    def _():
        fetch(own, 1)
        fetch(todo[0], 0)

    total[...] = jnp.zeros_like(total)

    @pl.when(pairs > 0)
    def _():
        arrived(1)
        turned[...] = held[1].T

    lane = lax.broadcasted_iota(jnp.int32, col_ref.shape, 1)
    column = jnp.sum(jnp.where(lane == own, col_ref[...], 0.0), axis=1, keepdims=True)

    def step(index, carry):
        buffer = lax.rem(index, 2)

        @pl.when(index + 1 < pairs)
        def _():
            fetch(todo[index + 1], lax.rem(index + 1, 2))

        arrived(buffer)
        slot = todo[index]
        energy = lambda which: occ_ref[slot_orbital(place_ref, count, occ_count, which)]
        shift = energy(own) + energy(slot)
        other = held[buffer]
        half = turned.shape[0] // 2
        halves = [slice(0, half), slice(half, 2 * half)]
        exchanges = [jnp.dot(turned[span, :], other, preferred_element_type=jnp.float32) for span in halves]
        for span, exchange in zip(halves, exchanges):
            denom = (column[span, :] + row_ref[slot]) - shift
            amplitude = (exchange / denom).astype(jnp.bfloat16)
            total[:, span] += lax.dot_general(
                other, amplitude, (((1,), (1,)), ((), ())), preferred_element_type=jnp.float32
            )
        return carry

    lax.fori_loop(0, pairs, step, jnp.int32(0))
    for index, out in enumerate(outs):
        out[...] = total[index * split : (index + 1) * split, :].astype(jnp.bfloat16)


def densities(rank, count, occ_count, live, codes, place, occ_energy, rows, own_vir, vir_rows, blocks):
    virs = own_vir.shape[0]
    aux = rows * count
    whole = lambda shape: pl.BlockSpec(shape, lambda: (0,) * len(shape))
    smem = pl.BlockSpec(memory_space=pltpu.SMEM)
    return pl.pallas_call(
        functools.partial(pair_kernel, rank, count, occ_count),
        in_specs=[smem] * 4
        + [whole(own_vir.shape), whole(vir_rows.shape)]
        + [pl.BlockSpec(memory_space=pl.ANY)] * len(blocks),
        out_specs=[whole((rows, virs))] * count,
        out_shape=[jax.ShapeDtypeStruct((rows, virs), jnp.bfloat16)] * count,
        scratch_shapes=[
            pltpu.VMEM((virs, aux), jnp.bfloat16),
            pltpu.VMEM((aux, virs), jnp.float32),
            pltpu.VMEM((2, aux, virs), jnp.bfloat16),
            pltpu.SemaphoreType.DMA((2, 2)),
            pltpu.SMEM((codes.shape[0],), jnp.int32),
        ],
        compiler_params=pltpu.CompilerParams(vmem_limit_bytes=20 * MIB),
        cost_estimate=pl.CostEstimate(
            flops=4 * 4 * aux * virs * virs, bytes_accessed=6 * aux * virs, transcendentals=0
        ),
        name="pairs",
    )(live, codes, place, occ_energy, own_vir, vir_rows, *blocks)


def spread_kernel(count, pos_ref, live_ref, code_ref, *refs):
    *pieces, out, where_ref = refs

    @pl.when(pl.program_id(0) == 0)
    def _():
        for owner in range(count):
            order = ranked(lambda slot: code_ref[owner, slot], live_ref[owner], code_ref.shape[1])
            for rank, orbital in enumerate(reversed(order)):
                where_ref[owner * OCC_DEV + rank] = owner * OCC_DEV + orbital

    orbitals = count * OCC_DEV
    width = orbitals * ROWS
    row = lax.broadcasted_iota(jnp.int32, (width, width), 0)
    col = lax.broadcasted_iota(jnp.int32, (width, width), 1)
    group = lax.broadcasted_iota(jnp.int32, (1, width), 1) // ROWS
    place = jnp.zeros((1, width), jnp.int32)
    for number in range(orbitals):
        owner = lax.rem(pos_ref[0] + number % count, count)
        place = jnp.where(group == number, where_ref[owner * OCC_DEV + number // count], place)
    hit = jnp.where((row % orbitals == place) & (row // orbitals == col % ROWS), 1.0, 0.0).astype(jnp.bfloat16)
    for part in range(out.shape[0] // ROWS):
        span = pl.ds(part * ROWS, ROWS)
        rows = jnp.concatenate([piece[span, :] for piece in pieces], axis=0)
        moved = jnp.dot(hit, rows, preferred_element_type=jnp.float32).astype(jnp.bfloat16)
        out[span] = moved.reshape(ROWS, orbitals, -1)


def assembled(pieces, aux_pos, count, live, codes):
    rows, virs = pieces[0].shape
    orbitals = count * OCC_DEV
    block = 4 * ROWS
    return pl.pallas_call(
        functools.partial(spread_kernel, count),
        grid_spec=pltpu.PrefetchScalarGridSpec(
            num_scalar_prefetch=3,
            grid=(rows // block,),
            in_specs=[pl.BlockSpec((block, virs), lambda g, *_: (g, 0))] * len(pieces),
            out_specs=pl.BlockSpec((block, orbitals, virs), lambda g, *_: (g, 0, 0)),
            scratch_shapes=[pltpu.SMEM((orbitals,), jnp.int32)],
        ),
        out_shape=jax.ShapeDtypeStruct((rows, orbitals, virs), jnp.bfloat16),
        compiler_params=pltpu.CompilerParams(vmem_limit_bytes=20 * MIB),
        cost_estimate=pl.CostEstimate(
            flops=2 * rows * orbitals * virs * orbitals * ROWS,
            bytes_accessed=4 * rows * orbitals * virs,
            transcendentals=0,
        ),
        name="assemble",
    )(aux_pos, live, codes, *pieces)


def body(half_ints, block_mask, vir_coef, domains, vir_energy, occ_energy, pair_count, pair_code):
    aux_count = lax.axis_size("aux")
    occ_count = lax.axis_size("occ")
    aux_pos = lax.axis_index("aux")
    occ_pos = lax.axis_index("occ")

    def along_aux(value, steps):
        return lax.ppermute(value, "aux", [(z, (z + steps) % aux_count) for z in range(aux_count)])

    rows_of, place = sorted_rows(
        half_ints, block_mask, aux_pos.astype(jnp.int32).reshape(1), occ_pos.astype(jnp.int32).reshape(1)
    )
    vir_rows, vir_cols = energies(place, domains, vir_energy, aux_count, occ_count)
    lists = lax.all_gather(jnp.concatenate([pair_code[0, 0], pair_count[0]]), "aux")
    twin, direct, far, last, late = routes(occ_count)
    transform = functools.partial(transformed, rows_of, domains, vir_coef, place, aux_count)

    order = list(range(1, aux_count)) + [0]
    sent = [None] * aux_count
    for step in order:
        sent[step] = transform(0, 0, step, 0, 1, [])[0]
    pieces = [sent[0]] + [along_aux(sent[step], step) for step in range(1, aux_count)]
    parts, owns, nears, thirds, lates, sets, swaps = [], [], [], [], [], [], []
    after = [sent[0]]
    for chunk in range(OCC_DEV + 1):
        coming = []
        if chunk + 1 < OCC_DEV:
            sent = transform(chunk + 1, 0, 0, 1, aux_count, after)
            coming = [sent[0]] + [along_aux(sent[step], step) for step in range(1, aux_count)]
        if chunk < OCC_DEV:
            parts.append(pieces)
            message = pieces[0 if chunk <= 1 else 1 :] + (coming[:1] if chunk >= 1 else [])
            rides = bool(last) and 0 < chunk < OCC_DEV - 1
            ready = nears[-1:] + ([] if rides else thirds[-1:]) + (coming[:1] if chunk == 0 else [])
            onward_rows = max(sum(piece.shape[0] for piece in message), owns[-1].shape[0]) if rides else 0
            own, *onward = stacked(message, place, thirds[-1:] if rides else [], ready, onward_rows)
            near = lax.ppermute(own, "occ", direct)
            third = lax.ppermute(onward[0], "occ", far + last) if rides else lax.ppermute(own, "occ", far)
            owns.append(own)
            nears.append(near)
            thirds.append(third)
            if rides:
                lates.append(third)
            if last and chunk >= OCC_DEV - 2:
                lates.append(lax.ppermute(third, "occ", last))
            if not last:
                lates.append(near)
        if chunk >= 1:
            waits = coming[1:] + nears[-1:] if coming else []
            both = with_next(owns[chunk - 1], nears[chunk - 1], lates[chunk - 1], late, place, waits)
            sets.append(both)
            swaps.append(lax.ppermute(both, "occ", twin))
        pieces, after = coming, [own, vir_rows]
    blocks = sets + swaps + thirds
    codes = pair_code[0, 0]
    results = []
    for turn in range(OCC_DEV):
        pieces = densities(
            OCC_DEV - 1 - turn, aux_count, occ_count, pair_count, codes, place, occ_energy, parts[0][0].shape[0],
            vir_cols, vir_rows, blocks,
        )
        results += [pieces[0]] + [along_aux(pieces[step], -step) for step in range(1, aux_count)]
    return assembled(results, place, aux_count, lists[:, -1], lists[:, :-1])


def routes(count):
    chips = count // 2
    twin = [(n, n ^ 1) for n in range(count)]
    turned = [c for c in range(0, chips, 2)] if chips == 4 else []
    direct = [(n, (n - 2) % count) for n in range(count) if n % 2 or n // 2 not in turned]
    far = [((n + 3) % count, n) for n in range(1, count, 2)]
    last = [(2 * ((c + 2) % chips) + 1, 2 * ((c - 1) % chips)) for c in turned]
    late = [target for _, target in last]
    return twin, direct, far, last, late


def solution(mesh):
    placed = (
        P("aux", "occ", None),
        P("aux", "occ"),
        P(),
        P(),
        P(),
        P(),
        P("occ", "aux"),
        P("occ", "aux", None),
    )
    return jax.shard_map(
        body, mesh=mesh, in_specs=placed, out_specs=P("aux", "occ", None), check_vma=False
    )
```

```python
import functools

import jax
import jax.numpy as jnp
from jax import lax
from jax.experimental import pallas as pl
from jax.experimental.pallas import tpu as pltpu
from jax.sharding import PartitionSpec as P

BLK = 64
OCC_DEV = 4
PARTNERS = 4
ROWS = 16
MIB = 1024 * 1024


def sort_kernel(mask_ref, aux_ref, occ_ref, x_ref, out_ref, place_ref):
    step = pl.program_id(0)
    block, orbitals, basis = x_ref.shape
    width = orbitals * ROWS
    place_ref[0] = aux_ref[0]
    place_ref[1] = occ_ref[0]
    row = lax.broadcasted_iota(jnp.int32, (ROWS, width), 0)
    col = lax.broadcasted_iota(jnp.int32, (ROWS, width), 1)
    spread = jnp.concatenate(
        [
            jnp.where(
                col == row * orbitals + orbital, mask_ref[step * block // BLK, orbital].astype(jnp.float32), 0.0
            )
            for orbital in range(orbitals)
        ],
        axis=0,
    ).astype(jnp.bfloat16)
    for part in range(block // ROWS):
        span = slice(part * ROWS, (part + 1) * ROWS)
        moved = jnp.dot(spread, x_ref[span].reshape(width, basis), preferred_element_type=jnp.float32)
        out_ref[:, span, :] = moved.astype(jnp.bfloat16).reshape(orbitals, ROWS, basis)


def sorted_rows(half_ints, block_mask, aux_pos, occ_pos):
    rows, orbitals, basis = half_ints.shape
    block = BLK
    smem = pl.BlockSpec(memory_space=pltpu.SMEM)
    return pl.pallas_call(
        sort_kernel,
        grid=(rows // block,),
        in_specs=[
            smem,
            smem,
            smem,
            pl.BlockSpec((block, orbitals, basis), lambda g: (g, 0, 0)),
        ],
        out_specs=[
            pl.BlockSpec((orbitals, block, basis), lambda g: (0, g, 0)),
            smem,
        ],
        out_shape=[
            jax.ShapeDtypeStruct((orbitals, rows, basis), jnp.bfloat16),
            jax.ShapeDtypeStruct((2,), jnp.int32),
        ],
        compiler_params=pltpu.CompilerParams(vmem_limit_bytes=40 * MIB),
        cost_estimate=pl.CostEstimate(
            flops=2 * rows * orbitals * basis * orbitals * ROWS,
            bytes_accessed=4 * rows * orbitals * basis,
            transcendentals=0,
        ),
        name="sort_rows",
    )(block_mask, aux_pos, occ_pos, half_ints)


def transform_kernel(count, orbitals, orbital, after, pos_ref, x_ref, dom_ref, coef_ref, *refs):
    out_refs = refs[after:]
    step = pl.program_id(0)
    tile = 512
    whole = coef_ref.shape[1]
    dom = dom_ref[pl.ds(pos_ref[1] * orbitals + orbital(step, pos_ref), 1), :]
    total = None
    for part in range(whole // tile):
        full = jnp.dot(
            x_ref[...], coef_ref[:, part * tile : (part + 1) * tile], preferred_element_type=jnp.float32
        ).astype(jnp.bfloat16)
        row = lax.broadcasted_iota(jnp.int32, (tile, dom.shape[1]), 0) + part * tile
        pick = jnp.where(row == dom, 1.0, 0.0).astype(jnp.bfloat16)
        term = jnp.dot(full, pick, preferred_element_type=jnp.float32)
        total = term if total is None else total + term
    total = total.astype(jnp.bfloat16)
    for index in range(count):
        @pl.when(step == index)
        def _():
            out_refs[index][...] = total


def transformed(rows_of, domains, vir_coef, place, aux_count, chunk, chunk_step, first, first_step, count, after):
    orbitals, rows, basis = rows_of.shape
    virs = domains.shape[1]
    whole = vir_coef.shape[1]

    def orbital(step, pos_ref):
        return lax.rem(pos_ref[0] + first + step * first_step, aux_count) * OCC_DEV + chunk + step * chunk_step

    return pl.pallas_call(
        functools.partial(transform_kernel, count, orbitals, orbital, len(after)),
        grid_spec=pltpu.PrefetchScalarGridSpec(
            num_scalar_prefetch=1,
            grid=(count,),
            in_specs=[
                pl.BlockSpec((None, rows, basis), lambda g, pos: (orbital(g, pos), 0, 0)),
                pl.BlockSpec(domains.shape, lambda g, pos: (0, 0)),
                pl.BlockSpec((basis, whole), lambda g, pos: (0, 0), pipeline_mode=pl.Buffered(1)),
            ]
            + [pl.BlockSpec(memory_space=pl.ANY)] * len(after),
            out_specs=[pl.BlockSpec((rows, virs), lambda g, pos: (0, 0)) for _ in range(count)],
        ),
        out_shape=[jax.ShapeDtypeStruct((rows, virs), jnp.bfloat16) for _ in range(count)],
        compiler_params=pltpu.CompilerParams(vmem_limit_bytes=20 * MIB),
        cost_estimate=pl.CostEstimate(
            flops=2 * count * rows * whole * (basis + virs),
            bytes_accessed=2 * (count * rows * (basis + virs) + basis * whole),
            transcendentals=0,
        ),
        name="transform",
    )(place, rows_of, domains, vir_coef, *after)


def join_kernel(count, place_ref, *refs):
    out = refs[count]
    rows = refs[0].shape[0]
    for index in range(count):
        out[index * rows : (index + 1) * rows, :] = refs[index][...]


def join_pass_kernel(count, place_ref, *refs):
    out, onward = refs[-2:]
    rows = refs[0].shape[0]
    for index in range(count):
        out[index * rows : (index + 1) * rows, :] = refs[index][...]

    @pl.when(place_ref[1] % 2 == 0)
    def _():
        onward[: count * rows, :] = out[...]
        if onward.shape[0] > count * rows:
            onward[count * rows :, :] = refs[count][count * rows : onward.shape[0], :]

    @pl.when(place_ref[1] % 2 == 1)
    def _():
        known = min(onward.shape[0], refs[count].shape[0])
        onward[:known, :] = refs[count][:known, :]
        if onward.shape[0] > known:
            onward[known:, :] = out[known : onward.shape[0], :]


def stacked(pieces, place, held, after, onward_rows=0):
    rows, virs = pieces[0].shape
    count = len(pieces)
    whole = pl.BlockSpec((count * rows, virs), lambda: (0, 0))
    shape = jax.ShapeDtypeStruct((count * rows, virs), pieces[0].dtype)
    kernel = join_pass_kernel if held else join_kernel
    outs = 1 + len(held)
    wide = [pl.BlockSpec((onward_rows, virs), lambda: (0, 0))] * len(held)

    def entry(place_ref, *refs):
        kernel(count, place_ref, *refs[: count + len(held)], *refs[-outs:])

    return pl.pallas_call(
        entry,
        in_specs=[pl.BlockSpec(memory_space=pltpu.SMEM)]
        + [pl.BlockSpec((rows, virs), lambda: (0, 0))] * count
        + [pl.BlockSpec(value.shape, lambda: (0, 0)) for value in held]
        + [pl.BlockSpec(memory_space=pl.ANY)] * len(after),
        out_specs=[whole] + wide,
        out_shape=[shape] + [jax.ShapeDtypeStruct((onward_rows, virs), pieces[0].dtype)] * len(held),
        compiler_params=pltpu.CompilerParams(vmem_limit_bytes=20 * MIB),
        cost_estimate=pl.CostEstimate(flops=0, bytes_accessed=4 * count * rows * virs * outs, transcendentals=0),
        name="join",
    )(place, *pieces, *held, *after)


def pick_kernel(late, place_ref, own_ref, near_ref, late_ref, *refs):
    out = refs[-1]
    is_late = functools.reduce(jnp.logical_or, [place_ref[1] == n for n in late], place_ref[1] < 0)
    out[0] = own_ref[...]

    @pl.when(jnp.logical_not(is_late))
    def _():
        out[1] = near_ref[...]

    @pl.when(is_late)
    def _():
        out[1] = late_ref[...]


def with_next(own, near, late_near, late, place, after):
    rows, virs = own.shape
    block = rows // 2
    return pl.pallas_call(
        functools.partial(pick_kernel, late),
        grid=(rows // block,),
        in_specs=[pl.BlockSpec(memory_space=pltpu.SMEM)]
        + [pl.BlockSpec((block, virs), lambda g: (g, 0))] * 3
        + [pl.BlockSpec(memory_space=pl.ANY)] * len(after),
        out_specs=pl.BlockSpec((2, block, virs), lambda g: (0, g, 0)),
        out_shape=jax.ShapeDtypeStruct((2, rows, virs), own.dtype),
        compiler_params=pltpu.CompilerParams(vmem_limit_bytes=16 * MIB),
        cost_estimate=pl.CostEstimate(flops=0, bytes_accessed=10 * rows * virs, transcendentals=0),
        name="pick",
    )(place, own, near, late_near, *after)


def slot_orbital(place_ref, aux_count, occ_count, slot):
    block = lax.rem(place_ref[1] + slot // OCC_DEV, occ_count) * aux_count + place_ref[0]
    return block * OCC_DEV + slot % OCC_DEV


def energy_kernel(aux_count, occ_count, place_ref, live_ref, code_ref, dom_ref, table_ref, row_ref, col_ref, order_ref):
    for rank, orbital in enumerate(ranked(lambda slot: code_ref[slot], live_ref[0, 0], code_ref.shape[0])):
        order_ref[rank] = orbital
    slots, _, virs = row_ref.shape
    lanes = table_ref.shape[1]
    rows = []
    for slot in range(slots):
        orbital = slot_orbital(place_ref, aux_count, occ_count, slot)
        rows.append(dom_ref[pl.ds(orbital, 1), :])
    doms = jnp.concatenate(rows, axis=0)
    for part in range(virs // lanes):
        span = slice(part * lanes, (part + 1) * lanes)
        dom = doms[:, span]
        high, low = dom // lanes, dom % lanes
        total = jnp.zeros((slots, lanes), jnp.float32)
        for line in range(table_ref.shape[0]):
            table = jnp.broadcast_to(table_ref[line : line + 1, :], (slots, lanes))
            found = jnp.take_along_axis(table, low, axis=1, mode="promise_in_bounds")
            total = jnp.where(high == line, found, total)
        row_ref[:, 0, span] = total
        col_ref[span, :] = total.T


def energies(place, live, codes, domains, vir_energy, aux_count, occ_count):
    slots, virs = PARTNERS * OCC_DEV, domains.shape[1]
    vmem, smem = pl.BlockSpec(memory_space=pltpu.VMEM), pl.BlockSpec(memory_space=pltpu.SMEM)
    return pl.pallas_call(
        functools.partial(energy_kernel, aux_count, occ_count),
        in_specs=[smem, smem, smem, vmem, vmem],
        out_specs=[vmem, vmem, smem],
        out_shape=[
            jax.ShapeDtypeStruct((slots, 1, virs), jnp.float32),
            jax.ShapeDtypeStruct((virs, slots), jnp.float32),
            jax.ShapeDtypeStruct((OCC_DEV,), jnp.int32),
        ],
        compiler_params=pltpu.CompilerParams(vmem_limit_bytes=8 * MIB),
        cost_estimate=pl.CostEstimate(flops=0, bytes_accessed=4 * domains.size, transcendentals=0),
        name="energies",
    )(place, live, codes, domains, vir_energy.reshape(-1, 128))


def ranked(code_at, live, slots):
    span = PARTNERS * OCC_DEV

    def tally(slot, counts):
        own = code_at(slot) // span
        return tuple(
            count + ((own == orbital) & (slot < live)).astype(jnp.int32) for orbital, count in enumerate(counts)
        )

    counts = lax.fori_loop(0, slots, tally, (jnp.int32(0),) * OCC_DEV)
    places = []
    for orbital, count in enumerate(counts):
        place = jnp.int32(0)
        for other, value in enumerate(counts):
            ahead = (value < count) | (value == count) if other < orbital else value < count
            place += ahead.astype(jnp.int32)
        places.append(place)
    return [
        sum(jnp.where(place == rank, orbital, 0) for orbital, place in enumerate(places)) for rank in range(OCC_DEV)
    ]


def pair_kernel(rank, count, occ_count, live_ref, code_ref, place_ref, occ_ref, col_ref, row_ref, *refs):
    sets = 3
    blocks = refs[: sets * OCC_DEV]
    outs = refs[sets * OCC_DEV : sets * OCC_DEV + count]
    turned, total, held, sems, todo = refs[sets * OCC_DEV + count :]
    aux = held.shape[1]
    split = aux // count
    span = PARTNERS * OCC_DEV
    slots = code_ref.shape[0]
    odd = place_ref[1] % 2
    own = ranked(lambda slot: code_ref[slot], live_ref[0, 0], slots)[rank]

    def scan(slot, found):
        code = code_ref[slot]
        mine = (slot < live_ref[0, 0]) & (code // span == own)

        @pl.when(mine)
        def _():
            todo[found] = code % span

        return found + mine.astype(jnp.int32)

    pairs = lax.fori_loop(0, slots, scan, jnp.int32(0))

    def source(slot):
        offset = slot // OCC_DEV
        one = jnp.where(odd == 1, 3, 2)
        three = jnp.where(odd == 1, 4, 3)
        kind = jnp.where(offset == 0, 0, jnp.where(offset == 1, one, jnp.where(offset == 2, 1, three)))
        return kind * OCC_DEV + slot % OCC_DEV

    def fetch(slot, buffer):
        place = source(slot)
        for kind in range(5):
            parts = [blocks[kind // 2 * OCC_DEV + orbital] for orbital in range(OCC_DEV)]
            parts = [part.at[kind % 2] for part in parts] if kind < 4 else parts
            for orbital in range(OCC_DEV):
                @pl.when(place == kind * OCC_DEV + orbital)
                def _():
                    if orbital <= 1:
                        first, rest = (parts[orbital].at[pl.ds(start, size)] for start, size in ((0, split), (split, aux - split)))
                    else:
                        start = aux if orbital == 2 else aux - split
                        first = parts[orbital - 1].at[pl.ds(start, split)]
                        rest = parts[orbital].at[pl.ds(0, aux - split)]
                    pltpu.make_async_copy(first, held.at[buffer, pl.ds(0, split)], sems.at[buffer, 0]).start()
                    pltpu.make_async_copy(rest, held.at[buffer, pl.ds(split, aux - split)], sems.at[buffer, 1]).start()

    def arrived(buffer):
        first, rest = held.at[buffer, pl.ds(0, split)], held.at[buffer, pl.ds(split, aux - split)]
        pltpu.make_async_copy(blocks[0].at[0, pl.ds(0, split)], first, sems.at[buffer, 0]).wait()
        pltpu.make_async_copy(blocks[0].at[0, pl.ds(split, aux - split)], rest, sems.at[buffer, 1]).wait()

    @pl.when(pairs > 0)
    def _():
        fetch(own, 1)
        fetch(todo[0], 0)

    total[...] = jnp.zeros_like(total)

    @pl.when(pairs > 0)
    def _():
        arrived(1)
        turned[...] = held[1].T

    lane = lax.broadcasted_iota(jnp.int32, col_ref.shape, 1)
    column = jnp.sum(jnp.where(lane == own, col_ref[...], 0.0), axis=1, keepdims=True)

    def step(index, carry):
        buffer = lax.rem(index, 2)

        @pl.when(index + 1 < pairs)
        def _():
            fetch(todo[index + 1], lax.rem(index + 1, 2))

        arrived(buffer)
        slot = todo[index]
        energy = lambda which: occ_ref[slot_orbital(place_ref, count, occ_count, which)]
        shift = energy(own) + energy(slot)
        other = held[buffer]
        half = turned.shape[0] // 2
        halves = [slice(0, half), slice(half, 2 * half)]
        exchanges = [jnp.dot(turned[span, :], other, preferred_element_type=jnp.float32) for span in halves]
        for span, exchange in zip(halves, exchanges):
            denom = (column[span, :] + row_ref[slot]) - shift
            amplitude = (exchange / denom).astype(jnp.bfloat16)
            total[:, span] += lax.dot_general(
                other, amplitude, (((1,), (1,)), ((), ())), preferred_element_type=jnp.float32
            )
        return carry

    lax.fori_loop(0, pairs, step, jnp.int32(0))
    for index, out in enumerate(outs):
        out[...] = total[index * split : (index + 1) * split, :].astype(jnp.bfloat16)


def densities(rank, count, occ_count, live, codes, place, occ_energy, rows, own_vir, vir_rows, blocks):
    virs = own_vir.shape[0]
    aux = rows * count
    whole = lambda shape: pl.BlockSpec(shape, lambda: (0,) * len(shape))
    smem = pl.BlockSpec(memory_space=pltpu.SMEM)
    return pl.pallas_call(
        functools.partial(pair_kernel, rank, count, occ_count),
        in_specs=[smem] * 4
        + [whole(own_vir.shape), whole(vir_rows.shape)]
        + [pl.BlockSpec(memory_space=pl.ANY)] * len(blocks),
        out_specs=[whole((rows, virs))] * count,
        out_shape=[jax.ShapeDtypeStruct((rows, virs), jnp.bfloat16)] * count,
        scratch_shapes=[
            pltpu.VMEM((virs, aux), jnp.bfloat16),
            pltpu.VMEM((aux, virs), jnp.float32),
            pltpu.VMEM((2, aux, virs), jnp.bfloat16),
            pltpu.SemaphoreType.DMA((2, 2)),
            pltpu.SMEM((codes.shape[0],), jnp.int32),
        ],
        compiler_params=pltpu.CompilerParams(vmem_limit_bytes=20 * MIB),
        cost_estimate=pl.CostEstimate(
            flops=4 * 4 * aux * virs * virs, bytes_accessed=6 * aux * virs, transcendentals=0
        ),
        name="pairs",
    )(live, codes, place, occ_energy, own_vir, vir_rows, *blocks)


def spread_kernel(count, pos_ref, order_ref, *refs):
    pieces, out = refs[:-1], refs[-1]
    orbitals = count * OCC_DEV
    width = orbitals * ROWS
    row = lax.broadcasted_iota(jnp.int32, (width, width), 0)
    col = lax.broadcasted_iota(jnp.int32, (width, width), 1)
    group = lax.broadcasted_iota(jnp.int32, (1, width), 1) // ROWS
    place = jnp.zeros((1, width), jnp.int32)
    for number in range(orbitals):
        owner = lax.rem(pos_ref[0] + number % count, count)
        orbital = owner * OCC_DEV + order_ref[owner, OCC_DEV - 1 - number // count]
        place = jnp.where(group == number, orbital, place)
    hit = jnp.where((row % orbitals == place) & (row // orbitals == col % ROWS), 1.0, 0.0).astype(jnp.bfloat16)
    for part in range(out.shape[0] // ROWS):
        span = pl.ds(part * ROWS, ROWS)
        rows = jnp.concatenate([piece[span, :] for piece in pieces], axis=0)
        moved = jnp.dot(hit, rows, preferred_element_type=jnp.float32).astype(jnp.bfloat16)
        out[span] = moved.reshape(ROWS, orbitals, -1)


def assembled(pieces, aux_pos, count, orders):
    rows, virs = pieces[0].shape
    orbitals = count * OCC_DEV
    block = 4 * ROWS
    return pl.pallas_call(
        functools.partial(spread_kernel, count),
        grid_spec=pltpu.PrefetchScalarGridSpec(
            num_scalar_prefetch=2,
            grid=(rows // block,),
            in_specs=[pl.BlockSpec((block, virs), lambda g, *_: (g, 0))] * len(pieces),
            out_specs=pl.BlockSpec((block, orbitals, virs), lambda g, *_: (g, 0, 0)),
        ),
        out_shape=jax.ShapeDtypeStruct((rows, orbitals, virs), jnp.bfloat16),
        compiler_params=pltpu.CompilerParams(vmem_limit_bytes=20 * MIB),
        cost_estimate=pl.CostEstimate(
            flops=2 * rows * orbitals * virs * orbitals * ROWS,
            bytes_accessed=4 * rows * orbitals * virs,
            transcendentals=0,
        ),
        name="assemble",
    )(aux_pos, orders, *pieces)


def body(half_ints, block_mask, vir_coef, domains, vir_energy, occ_energy, pair_count, pair_code):
    aux_count = lax.axis_size("aux")
    occ_count = lax.axis_size("occ")
    aux_pos = lax.axis_index("aux")
    occ_pos = lax.axis_index("occ")

    def along_aux(value, steps):
        return lax.ppermute(value, "aux", [(z, (z + steps) % aux_count) for z in range(aux_count)])

    rows_of, place = sorted_rows(
        half_ints, block_mask, aux_pos.astype(jnp.int32).reshape(1), occ_pos.astype(jnp.int32).reshape(1)
    )
    codes = pair_code[0, 0]
    vir_rows, vir_cols, order = energies(place, pair_count, codes, domains, vir_energy, aux_count, occ_count)
    orders = lax.all_gather(order, "aux")
    twin, direct, far, last, late = routes(occ_count)
    transform = functools.partial(transformed, rows_of, domains, vir_coef, place, aux_count)

    order = list(range(1, aux_count)) + [0]
    sent = [None] * aux_count
    for step in order:
        sent[step] = transform(0, 0, step, 0, 1, [])[0]
    pieces = [sent[0]] + [along_aux(sent[step], step) for step in range(1, aux_count)]
    parts, owns, nears, thirds, lates, sets, swaps = [], [], [], [], [], [], []
    after = [sent[0]]
    for chunk in range(OCC_DEV + 1):
        coming = []
        if chunk + 1 < OCC_DEV:
            sent = transform(chunk + 1, 0, 0, 1, aux_count, after)
            coming = [sent[0]] + [along_aux(sent[step], step) for step in range(1, aux_count)]
        if chunk < OCC_DEV:
            parts.append(pieces)
            message = pieces[0 if chunk <= 1 else 1 :] + (coming[:1] if chunk >= 1 else [])
            rides = bool(last) and 0 < chunk < OCC_DEV - 1
            ready = nears[-1:] + ([] if rides else thirds[-1:]) + (coming[:1] if chunk == 0 else [])
            onward_rows = max(sum(piece.shape[0] for piece in message), owns[-1].shape[0]) if rides else 0
            own, *onward = stacked(message, place, thirds[-1:] if rides else [], ready, onward_rows)
            near = lax.ppermute(own, "occ", direct)
            third = lax.ppermute(onward[0], "occ", far + last) if rides else lax.ppermute(own, "occ", far)
            owns.append(own)
            nears.append(near)
            thirds.append(third)
            if rides:
                lates.append(third)
            if last and chunk >= OCC_DEV - 2:
                lates.append(lax.ppermute(third, "occ", last))
            if not last:
                lates.append(near)
        if chunk >= 1:
            waits = coming[1:] + nears[-1:] if coming else []
            both = with_next(owns[chunk - 1], nears[chunk - 1], lates[chunk - 1], late, place, waits)
            sets.append(both)
            swaps.append(lax.ppermute(both, "occ", twin))
        pieces, after = coming, [own, vir_rows]
    blocks = sets + swaps + thirds
    codes = pair_code[0, 0]
    results = []
    for turn in range(OCC_DEV):
        pieces = densities(
            OCC_DEV - 1 - turn, aux_count, occ_count, pair_count, codes, place, occ_energy, parts[0][0].shape[0],
            vir_cols, vir_rows, blocks,
        )
        results += [pieces[0]] + [along_aux(pieces[step], -step) for step in range(1, aux_count)]
    return assembled(results, place, aux_count, orders)


def routes(count):
    chips = count // 2
    twin = [(n, n ^ 1) for n in range(count)]
    turned = [c for c in range(0, chips, 2)] if chips == 4 else []
    direct = [(n, (n - 2) % count) for n in range(count) if n % 2 or n // 2 not in turned]
    far = [((n + 3) % count, n) for n in range(1, count, 2)]
    last = [(2 * ((c + 2) % chips) + 1, 2 * ((c - 1) % chips)) for c in turned]
    late = [target for _, target in last]
    return twin, direct, far, last, late


def solution(mesh):
    placed = (
        P("aux", "occ", None),
        P("aux", "occ"),
        P(),
        P(),
        P(),
        P(),
        P("occ", "aux"),
        P("occ", "aux", None),
    )
    return jax.shard_map(
        body, mesh=mesh, in_specs=placed, out_specs=P("aux", "occ", None), check_vma=False
    )
```
